128 devices in a mesh: dp: 8 (over y, core), seq: 16 (over x, z).
Axes of the slice: x: 4, y: 4, z: 4, core: 2. Of those that a mesh axis runs over, the one named last changes fastest.
Arguments:
- nodes: bfloat16 [8, 2048, 1024], P('dp', 'seq'), may hold values from -6 to 6
- w_qkv: bfloat16 [1024, 3072], replicated, as said below
- w_out: bfloat16 [1024, 1024], replicated, may hold values from -0.1875 to 0.1875
- cotangent: bfloat16 [8, 2048, 1024], P('dp', 'seq'), may hold values from -6 to 6
- order: int32 [8, 2048], P('dp'), may hold values from 0 to 2047, each once within a row
- block_list: int32 [8, 32, 8], P('dp'), may hold values from 0 to 31, as said below
- block_count: int32 [8, 32], P('dp'), may hold values from 1 to 8, as said below
Outputs:
- mixed: bfloat16 [8, 2048, 1024], P('dp', 'seq')
- grad_nodes: bfloat16 [8, 2048, 1024], P('dp', 'seq')
- grad_qkv: float32 [1024, 3072], P(('dp', 'seq'))
- grad_out: float32 [1024, 1024], P(('dp', 'seq'))
The draws below stay inside these ranges and needn't reach their ends.
Inputs may be any that keep to these rules, and one draw needn't show every extreme that they name: Columns of w_qkv are ordered by head, then query, key, value, then the head's 64 features. `block_list`: each row lists 8 different key blocks, the first being the query block itself; only the first block_count entries are used. `block_count`: in every batch some query block uses all 8 entries.
All inputs are finite; a program needn't handle non-finite values.
Results may differ from the reference program's by a relative error of at most 0.017.
Values may be sent and summed in bfloat16 or wider, within the bound.
No kernel may reach another device: no remote copies, remote signals or barrier semaphores. Data moves between devices by JAX's collectives and lax.ppermute only.
A program may use at most 128 MiB of HBM per device.

```python
import math
import jax
import jax.numpy as jnp
from jax import lax

H = 16
HD = 64
D = 1024
BLK = 64
MAXB = 8
GROUP = 8
NODES = 2048
NBLK = 32
BATCHES = 8


def draw_w_qkv(key, part):
    key = jax.random.fold_in(key, 13)
    first = jax.random.fold_in(key, 0)
    sample_all = jax.random.normal(first, (D, H, 3, HD), jnp.float32) / math.sqrt(D)
    return sample_all.reshape(D, 3 * D).astype(jnp.bfloat16)


def draw_block_list(key, part):
    key = jax.random.fold_in(key, 11)
    seeds = jax.random.split(key, BATCHES * NBLK)

    def offsets_for(single_key):
        others = jax.random.permutation(single_key, NBLK - 1)[:MAXB - 1] + 1
        return jnp.concatenate([jnp.zeros((1,), jnp.int32), others.astype(jnp.int32)])
    offsets = jax.vmap(offsets_for)(seeds).reshape(BATCHES, NBLK, MAXB)
    itself = jnp.arange(NBLK, dtype=jnp.int32)[None, :, None]
    return ((itself + offsets) % NBLK).astype(jnp.int32)


def draw_block_count(key, part):
    key = jax.random.fold_in(key, 12)
    first, second = jax.random.split(key)
    counts = jax.random.randint(first, (BATCHES, NBLK), 1, MAXB + 1)
    fullest = jax.random.randint(second, (BATCHES, 1), 0, NBLK)
    return jnp.where(jnp.arange(NBLK)[None, :] == fullest, MAXB, counts).astype(jnp.int32)


def raised(values, key, source, target, parts, factor):
    owner, partner = [(jnp.arange(values.shape[dim]) // (values.shape[dim] // parts)).reshape([-1 if axis == dim else 1 for axis in range(values.ndim)]) for dim in (source, target)]
    chosen = jax.random.permutation(key, parts)[partner]
    strong = (owner == chosen) | (owner == (partner + parts // 2) % parts)
    return jnp.where(strong, factor * values, values)


def block_levels(own_key, extent, shards, smallest, high):
    def one(dim, parts):
        draws = jax.random.uniform(jax.random.fold_in(jax.random.fold_in(own_key, 6), dim), (parts,), jnp.float32, smallest / len(shards), high / len(shards))
        return jnp.repeat(jnp.exp(draws), extent[dim] // parts).reshape((-1,) + (1,) * (len(extent) - dim - 1))

    gain = one(*shards[0])
    for cut in shards[1:]:
        gain = gain * one(*cut)
    return gain


def noise(stream_key, extent, scale, most, cuts=(), kind=jnp.bfloat16):
    level = block_levels(stream_key, extent, cuts, -0.22, 0.18) if cuts else 1.0
    values = jax.random.normal(stream_key, extent, jnp.float32) * scale * level
    return jnp.minimum(jnp.maximum(values, -most), most).astype(kind)


def bell_draw_with(own_key, extent, scale, reach, shards, heavy, kind=jnp.bfloat16):
    drawn = scale * jax.random.normal(own_key, extent, jnp.float32)
    if shards:
        drawn = drawn * block_levels(own_key, extent, shards, -0.22, 0.18)
    return jnp.clip(raised(drawn, jax.random.fold_in(own_key, 3), *heavy), -reach, reach).astype(kind)


def setup_inputs(seed: int = 0) -> dict:
    arg_keys = jax.random.split(jax.random.key(seed), 8)
    nodes = bell_draw_with(arg_keys[0], (BATCHES, NODES, D), 1.0, 6.0, ((0, 8), (1, 16)), (1, 2, 16, 2.0))
    w_qkv = draw_w_qkv(jax.random.fold_in(arg_keys[7], 71), 0)
    w_out = noise(arg_keys[2], (D, D), D ** -0.5, 0.1875)
    cotangent = noise(arg_keys[3], (BATCHES, NODES, D), 1.0, 6.0, ((0, 8), (1, 16)))
    order = jax.vmap(lambda own: jax.random.permutation(own, NODES))(jax.random.split(arg_keys[4], BATCHES)).reshape((BATCHES, NODES)).astype(jnp.int32)
    block_list = draw_block_list(jax.random.fold_in(arg_keys[7], 71), 0)
    block_count = draw_block_count(jax.random.fold_in(arg_keys[7], 71), 0)
    return dict(nodes=nodes, w_qkv=w_qkv, w_out=w_out, cotangent=cotangent, order=order, block_list=block_list, block_count=block_count)


EPS = 1e-05

def fetch_blocks(source, chosen):
    gathered = source[chosen]
    return gathered.reshape(chosen.shape[0], chosen.shape[1] * source.shape[1], source.shape[2])

def block_probs(queries, keyed, tally, scale):
    scores = jnp.einsum('gqe,gke->gqk', queries.astype(jnp.float32), keyed.astype(jnp.float32)) * scale
    usable = jnp.arange(MAXB)[None, :] < tally[:, None]
    usable = jnp.repeat(usable, BLK, axis=1)[:, None, :]
    scores = jnp.where(usable, scores, jnp.float32(-1e+30))
    highest = lax.optimization_barrier(jnp.max(scores, axis=-1, keepdims=True))
    expo = jnp.exp(scores - highest)
    return expo / lax.optimization_barrier(jnp.sum(expo, axis=-1, keepdims=True))

def head_forward(queries, keys_all, values_all, picked, counted):
    nblk = picked.shape[0]
    width = queries.shape[1]
    scale = 1.0 / math.sqrt(width)
    key_table = keys_all.reshape(nblk, BLK, width)
    value_table = values_all.reshape(nblk, BLK, width)
    query_groups = queries.reshape(nblk // GROUP, GROUP, BLK, width)

    def per_group(packed_in):
        query_block, chosen, tally = packed_in
        keyed = fetch_blocks(key_table, chosen)
        valued = fetch_blocks(value_table, chosen)
        probs = block_probs(query_block, keyed, tally, scale)
        probs_low = lax.optimization_barrier(probs.astype(jnp.bfloat16))
        result = jnp.einsum('gqk,gke->gqe', probs_low.astype(jnp.float32), valued.astype(jnp.float32))
        return result.astype(jnp.bfloat16)
    outputs = lax.map(per_group, (query_groups, picked.reshape(nblk // GROUP, GROUP, MAXB), counted.reshape(nblk // GROUP, GROUP)))
    return outputs.reshape(nblk * BLK, width)

def head_backward(queries, keys_all, values_all, grad_in, picked, counted):
    nblk = picked.shape[0]
    width = queries.shape[1]
    scale = 1.0 / math.sqrt(width)
    key_table = keys_all.reshape(nblk, BLK, width)
    value_table = values_all.reshape(nblk, BLK, width)
    query_groups = queries.reshape(nblk // GROUP, GROUP, BLK, width)
    grad_groups = grad_in.reshape(nblk // GROUP, GROUP, BLK, width)

    def per_group(carry, packed_in):
        key_acc, value_acc = carry
        query_block, grad_block, chosen, tally = packed_in
        keyed = fetch_blocks(key_table, chosen)
        valued = fetch_blocks(value_table, chosen)
        probs = block_probs(query_block, keyed, tally, scale)
        probs_low = lax.optimization_barrier(probs.astype(jnp.bfloat16))
        grad_probs = jnp.einsum('gqe,gke->gqk', grad_block.astype(jnp.float32), valued.astype(jnp.float32))
        delta = lax.optimization_barrier(jnp.sum(grad_probs * probs, axis=-1, keepdims=True))
        grad_scores = lax.optimization_barrier((probs * (grad_probs - delta) * scale).astype(jnp.bfloat16))
        grad_query = jnp.einsum('gqk,gke->gqe', grad_scores.astype(jnp.float32), keyed.astype(jnp.float32)).astype(jnp.bfloat16)
        key_part = jnp.einsum('gqk,gqe->gke', grad_scores.astype(jnp.float32), query_block.astype(jnp.float32))
        value_part = jnp.einsum('gqk,gqe->gke', probs_low.astype(jnp.float32), grad_block.astype(jnp.float32))
        flat = chosen.reshape(-1)
        key_acc = key_acc.at[flat].add(key_part.reshape(-1, BLK, width))
        value_acc = value_acc.at[flat].add(value_part.reshape(-1, BLK, width))
        return ((key_acc, value_acc), grad_query)
    start_acc = jnp.zeros((nblk, BLK, width), jnp.float32)
    (key_acc, value_acc), grad_queries = lax.scan(per_group, (start_acc, start_acc), (query_groups, grad_groups, picked.reshape(nblk // GROUP, GROUP, MAXB), counted.reshape(nblk // GROUP, GROUP)))
    grad_queries = grad_queries.reshape(nblk * BLK, width)
    grad_keys = key_acc.reshape(nblk * BLK, width).astype(jnp.bfloat16)
    grad_values = value_acc.reshape(nblk * BLK, width).astype(jnp.bfloat16)
    return jnp.concatenate([grad_queries, grad_keys, grad_values], axis=1)

def attend_all(clustered, picked, counted):
    width = clustered.shape[2] // 3
    per_head = jnp.moveaxis(clustered, 1, 0)

    def single(head_rows):
        return head_forward(head_rows[:, :width], head_rows[:, width:2 * width], head_rows[:, 2 * width:], picked, counted)
    return jnp.moveaxis(lax.map(single, per_head), 0, 1)

def attend_back(clustered, grad_cluster, picked, counted):
    width = clustered.shape[2] // 3
    per_head = (jnp.moveaxis(clustered, 1, 0), jnp.moveaxis(grad_cluster, 1, 0))

    def single(pair):
        head_rows, head_grad = pair
        return head_backward(head_rows[:, :width], head_rows[:, width:2 * width], head_rows[:, 2 * width:], head_grad, picked, counted)
    return jnp.moveaxis(lax.map(single, per_head), 0, 1)

def reference(nodes, w_qkv, w_out, cotangent, order, block_list, block_count):
    contract_rows = (((0,), (0,)), ((), ()))
    contract_cols = (((1,), (1,)), ((), ()))

    def per_batch(carry, packed_in):
        features, upstream, ordering, picked, counted = packed_in
        wide_in = features.astype(jnp.float32)
        inv_rms = lax.rsqrt(lax.optimization_barrier(jnp.mean(wide_in * wide_in, axis=-1, keepdims=True)) + EPS)
        normed = (wide_in * inv_rms).astype(jnp.bfloat16)
        packed = jnp.dot(normed, w_qkv, preferred_element_type=jnp.float32).astype(jnp.bfloat16).reshape(NODES, H, 3 * HD)
        inverse = jnp.zeros((NODES,), jnp.int32).at[ordering].set(jnp.arange(NODES, dtype=jnp.int32))
        clustered = packed[ordering]
        attn = attend_all(clustered, picked, counted)[inverse].reshape(NODES, D)
        mixed = (wide_in + jnp.dot(attn, w_out, preferred_element_type=jnp.float32)).astype(jnp.bfloat16)
        grad_attn = lax.dot_general(upstream, w_out, contract_cols, preferred_element_type=jnp.float32).astype(jnp.bfloat16).reshape(NODES, H, HD)
        grad_packed = attend_back(clustered, grad_attn[ordering], picked, counted)[inverse].reshape(NODES, 3 * D)
        grad_normed = lax.dot_general(grad_packed, w_qkv, contract_cols, preferred_element_type=jnp.float32)
        inner = lax.optimization_barrier(jnp.mean(grad_normed * wide_in, axis=-1, keepdims=True))
        grad_features = (upstream.astype(jnp.float32) + inv_rms * grad_normed - wide_in * inv_rms * inv_rms * inv_rms * inner).astype(jnp.bfloat16)
        qkv_sum = carry[0] + lax.dot_general(normed, grad_packed, contract_rows, preferred_element_type=jnp.float32)
        out_sum = carry[1] + lax.dot_general(attn, upstream, contract_rows, preferred_element_type=jnp.float32)
        return ((qkv_sum, out_sum), (mixed, grad_features))
    start_sums = (jnp.zeros((D, 3 * D), jnp.float32), jnp.zeros((D, D), jnp.float32))
    (grad_qkv, grad_out), (mixed, grad_nodes) = lax.scan(per_batch, start_sums, (nodes, cotangent, order, block_list, block_count))
    return (mixed, grad_nodes, grad_qkv, grad_out)
```

```python
import functools
import math

import jax
import jax.numpy as jnp
from jax import lax
from jax.experimental import pallas as pl
from jax.experimental.pallas import tpu as pltpu
from jax.sharding import PartitionSpec as P

H = 16
HD = 64
D = 1024
BLK = 64
MAXB = 8
NODES = 2048
NBLK = 32
WIDE = 4 * HD
TILE = 256
EPS = 1e-05
SCALE = 1.0 / math.sqrt(HD)


def contract(a, b, da, db):
    return lax.dot_general(a, b, (((da,), (db,)), ((), ())), preferred_element_type=jnp.float32)


def attention_kernel(list_ref, count_ref, order_ref, rows_ref, out_ref, qg_ref, kv_ref, acc_ref, res_ref):
    low_lanes = lax.broadcasted_iota(jnp.int32, (TILE, 2 * HD), 1) < HD

    def to_cluster(t, carry):
        start = pl.multiple_of(t * TILE, TILE)
        ordered = jnp.broadcast_to(order_ref[:, pl.ds(start, TILE)], (128, TILE))
        position = jnp.transpose(ordered.astype(jnp.float32)).astype(jnp.int32)
        lanes = lax.broadcasted_iota(jnp.int32, (TILE, 128), 1)
        pick = jnp.concatenate(
            [(position == lanes + 128 * c).astype(jnp.float32).astype(jnp.bfloat16) for c in range(NODES // 128)],
            axis=1,
        )
        moved = contract(pick, rows_ref[...], 1, 0)
        first, second = moved[:, : 2 * HD], moved[:, 2 * HD :]
        qg_ref[pl.ds(start, TILE), :] = jnp.where(low_lanes, first, second).astype(jnp.bfloat16)
        kv_ref[pl.ds(start, TILE), :] = jnp.where(
            low_lanes, pltpu.roll(first, HD, 1), pltpu.roll(second, HD, 1)
        ).astype(jnp.bfloat16)
        return carry

    lax.fori_loop(0, NODES // TILE, to_cluster, 0)
    acc_ref[...] = jnp.zeros_like(acc_ref)
    block_low = lax.broadcasted_iota(jnp.int32, (BLK, 2 * HD), 1) < HD
    key_slot = lax.broadcasted_iota(jnp.int32, (BLK, MAXB * BLK), 1) // BLK

    def per_block(b, carry):
        start = pl.multiple_of(b * BLK, BLK)
        qg = qg_ref[pl.ds(start, BLK), :].astype(jnp.float32)
        keys_at = [pl.multiple_of(list_ref[b, j] * BLK, BLK) for j in range(MAXB)]
        kv = jnp.concatenate([kv_ref[pl.ds(at, BLK), :] for at in keys_at], axis=0)
        zero = jnp.zeros_like(qg)
        split = jnp.concatenate(
            [jnp.where(block_low, qg, zero), jnp.where(block_low, zero, qg)], axis=0
        ).astype(jnp.bfloat16)
        both = contract(split, kv, 1, 1)
        scores = jnp.where(key_slot < count_ref[b], both[:BLK] * SCALE, jnp.float32(-1e30))
        expo = jnp.exp(scores - jnp.max(scores, axis=1, keepdims=True))
        probs = expo * (1.0 / jnp.sum(expo, axis=1, keepdims=True))
        grad_probs = both[BLK:]
        delta = jnp.sum(grad_probs * probs, axis=1, keepdims=True)
        grad_scores = probs * (grad_probs - delta) * SCALE
        stacked = jnp.concatenate([grad_scores, probs], axis=0).astype(jnp.bfloat16)
        crossed = contract(stacked, kv, 1, 0)
        res_ref[pl.ds(start, BLK), :] = jnp.where(block_low, crossed[:BLK], crossed[BLK:])
        parts = contract(stacked, split, 0, 0)
        for j in range(MAXB):
            acc_ref[pl.ds(keys_at[j], BLK), :] += parts[j * BLK : (j + 1) * BLK]
        return carry

    lax.fori_loop(0, NBLK, per_block, 0)

    def assemble(t, carry):
        start = pl.multiple_of(t * TILE, TILE)
        dqo = res_ref[pl.ds(start, TILE), :]
        turned = pltpu.roll(acc_ref[pl.ds(start, TILE), :], HD, 1)
        qg_ref[pl.ds(start, TILE), :] = jnp.where(low_lanes, dqo, turned).astype(jnp.bfloat16)
        kv_ref[pl.ds(start, TILE), :] = jnp.where(low_lanes, turned, dqo).astype(jnp.bfloat16)
        return carry

    lax.fori_loop(0, NODES // TILE, assemble, 0)

    def to_nodes(t, carry):
        start = pl.multiple_of(t * TILE, TILE)
        node = lax.broadcasted_iota(jnp.int32, (TILE, NODES), 0) + start
        pick = (node == order_ref[...]).astype(jnp.float32).astype(jnp.bfloat16)
        out_ref[pl.ds(start, TILE), : 2 * HD] = contract(pick, qg_ref[...], 1, 0).astype(jnp.bfloat16)
        out_ref[pl.ds(start, TILE), 2 * HD :] = contract(pick, kv_ref[...], 1, 0).astype(jnp.bfloat16)
        return carry

    lax.fori_loop(0, NODES // TILE, to_nodes, 0)


def attention(picked, counted, order, rows):
    return pl.pallas_call(
        attention_kernel,
        out_shape=jax.ShapeDtypeStruct((NODES, WIDE), jnp.bfloat16),
        in_specs=[
            pl.BlockSpec(memory_space=pltpu.SMEM),
            pl.BlockSpec(memory_space=pltpu.SMEM),
            pl.BlockSpec(memory_space=pltpu.VMEM),
            pl.BlockSpec(memory_space=pltpu.VMEM),
        ],
        out_specs=pl.BlockSpec(memory_space=pltpu.VMEM),
        scratch_shapes=[
            pltpu.VMEM((NODES, 2 * HD), jnp.bfloat16),
            pltpu.VMEM((NODES, 2 * HD), jnp.bfloat16),
            pltpu.VMEM((NODES, 2 * HD), jnp.float32),
            pltpu.VMEM((NODES, 2 * HD), jnp.float32),
        ],
        compiler_params=pltpu.CompilerParams(vmem_limit_bytes=40 * 1024 * 1024),
        cost_estimate=pl.CostEstimate(flops=10_000_000_000, bytes_accessed=4_000_000, transcendentals=1_000_000),
        name="clustered_attention",
    )(picked, counted, order, rows)


def shards(nodes, w_qkv, w_out, cotangent, order, block_list, block_count):
    features = nodes[0]
    upstream = cotangent[0]
    rows = features.shape[0]
    wide_in = features.astype(jnp.float32)
    inv_rms = lax.rsqrt(jnp.mean(wide_in * wide_in, axis=-1, keepdims=True) + EPS)
    normed = (wide_in * inv_rms).astype(jnp.bfloat16)
    all_normed = lax.all_gather(normed, "seq", axis=0, tiled=True)
    all_upstream = lax.all_gather(upstream, "seq", axis=0, tiled=True)
    packed = contract(normed, w_qkv, 1, 0).astype(jnp.bfloat16).reshape(rows, H, 3 * HD)
    projected = contract(upstream, w_out, 1, 1).astype(jnp.bfloat16).reshape(rows, H, HD)
    sent = jnp.concatenate([packed, projected], axis=2).transpose(1, 0, 2)
    head_rows = lax.all_to_all(sent, "seq", 0, 0, tiled=True).reshape(NODES, WIDE)
    head_out = attention(block_list[0], block_count[0], order, head_rows)

    part_qkv = contract(all_normed, head_out[:, : 3 * HD], 0, 0)
    part_out = contract(head_out[:, 3 * HD :], all_upstream, 0, 0)
    parts = jnp.concatenate(
        [part_qkv.reshape(8, 128 * 3 * HD), part_out.reshape(8, 8 * D)], axis=1
    ).astype(jnp.bfloat16).reshape(8, 128, WIDE)
    batches = lax.all_to_all(parts, "dp", 0, 0, tiled=True)
    total = jnp.sum(batches.astype(jnp.float32), axis=0).reshape(128 * WIDE)
    head_qkv = total[: 128 * 3 * HD].reshape(H, 8, 3 * HD)
    head_rows_out = total[128 * 3 * HD :].reshape(8, D)
    grad_qkv = lax.all_to_all(head_qkv, "seq", 0, 0, tiled=True).transpose(1, 0, 2).reshape(8, 3 * D)
    moves = [(i * H + h, h * 8 + i) for i in range(8) for h in range(H)]
    grad_out = lax.ppermute(head_rows_out, ("dp", "seq"), moves)

    back = lax.all_to_all(head_out.reshape(H, rows, WIDE), "seq", 0, 0, tiled=True).transpose(1, 0, 2)
    grad_packed = back[:, :, : 3 * HD].reshape(rows, 3 * D)
    attn = back[:, :, 3 * HD :].reshape(rows, D)
    mixed = (wide_in + contract(attn, w_out, 1, 0)).astype(jnp.bfloat16)
    grad_normed = contract(grad_packed, w_qkv, 1, 1)
    inner = jnp.mean(grad_normed * wide_in, axis=-1, keepdims=True)
    grad_nodes = (
        upstream.astype(jnp.float32)
        + inv_rms * grad_normed
        - wide_in * inv_rms * inv_rms * inv_rms * inner
    ).astype(jnp.bfloat16)
    return mixed[None], grad_nodes[None], grad_qkv, grad_out


def solution(mesh):
    return jax.shard_map(
        shards,
        mesh=mesh,
        in_specs=(
            P("dp", "seq", None),
            P(),
            P(),
            P("dp", "seq", None),
            P("dp", None),
            P("dp", None, None),
            P("dp", None),
        ),
        out_specs=(
            P("dp", "seq", None),
            P("dp", "seq", None),
            P(("dp", "seq"), None),
            P(("dp", "seq"), None),
        ),
        check_vma=False,
    )
```

```python
import math

import jax
import jax.numpy as jnp
from jax import lax
from jax.experimental import pallas as pl
from jax.experimental.pallas import tpu as pltpu
from jax.sharding import PartitionSpec as P

H = 16
HD = 64
D = 1024
BLK = 64
MAXB = 8
NODES = 2048
NBLK = 32
WIDE = 4 * HD
TILE = 2048
PAIRS = 2
STEPS = (8, 4)
DP = 8
SEQ = 16
ROWS = 128
CHUNK = 512
HALF = ROWS // 2
VMEM_BYTES = 60 * 1024 * 1024
EPS = 1e-05
SCALE = 1.0 / math.sqrt(HD)


def contract(a, b, da, db):
    return lax.dot_general(a, b, (((da,), (db,)), ((), ())), preferred_element_type=jnp.float32)


def attention_kernel(
    list_ref, count_ref, ranked_ref, bounds_ref, order_ref, rows_ref, after_ref, out_ref, attn_ref, grads_ref, qg_ref, kv_ref, acc_ref, done_ref, both_ref
):
    low_lanes = lax.broadcasted_iota(jnp.int32, (TILE, 2 * HD), 1) < HD
    one, none = jnp.ones((TILE, 128), jnp.bfloat16), jnp.zeros((TILE, 128), jnp.bfloat16)

    def to_cluster(t, carry):
        start = pl.multiple_of(t * TILE, TILE)
        ordered = jnp.broadcast_to(order_ref[:, pl.ds(start, TILE)], (128, TILE))
        position = jnp.transpose(ordered.astype(jnp.float32)).astype(jnp.int32)
        lanes = lax.broadcasted_iota(jnp.int32, (TILE, 128), 1)
        within = (position % 128 == lanes).astype(jnp.float32).astype(jnp.bfloat16)
        tile_of = (position // 128).astype(jnp.float32).astype(jnp.bfloat16)
        pick = jnp.concatenate(
            [jnp.where(tile_of == jnp.bfloat16(c), within, none) for c in range(NODES // 128)], axis=1
        )
        moved = contract(pick, rows_ref[...], 1, 0)
        first, second = moved[:, : 2 * HD], moved[:, 2 * HD :]
        qg_ref[pl.ds(start, TILE), :] = jnp.where(low_lanes, first * SCALE, second).astype(jnp.bfloat16)
        kv_ref[pl.ds(start, TILE), :] = jnp.where(
            low_lanes, pltpu.roll(first, HD, 1), pltpu.roll(second, HD, 1)
        ).astype(jnp.bfloat16)
        return carry

    lax.fori_loop(0, NODES // TILE, to_cluster, 0)
    acc_ref[...] = jnp.zeros_like(acc_ref)
    block_low = lax.broadcasted_iota(jnp.int32, (BLK, 2 * HD), 1) < HD
    pair_low = lax.broadcasted_iota(jnp.int32, (1, 2 * BLK), 1) < BLK

    def folded(parts, op):
        total = parts[0]
        for part in parts[1:]:
            total = op(total, part)
        return total

    def pair(at, slot, used):
        blocks = (ranked_ref[at], ranked_ref[at + 1])
        starts = [pl.multiple_of(b * BLK, BLK) for b in blocks]
        qg = [qg_ref[pl.ds(s, BLK), :].astype(jnp.float32) for s in starts]
        keys_at = [[pl.multiple_of(list_ref[b, j] * BLK, BLK) for j in range(used)] for b in blocks]
        kv = jnp.concatenate(
            [jnp.concatenate([kv_ref[pl.ds(key, BLK), :] for key in keys], axis=0) for keys in keys_at], axis=1
        )
        zero = jnp.zeros_like(qg[0])
        q0, q1 = (jnp.where(block_low, x, zero) for x in qg)
        g0, g1 = (jnp.where(block_low, zero, x) for x in qg)
        split = jnp.concatenate(
            [
                jnp.concatenate([q0, zero, g0, zero], axis=0),
                jnp.concatenate([zero, q1, zero, g1], axis=0),
            ],
            axis=1,
        ).astype(jnp.bfloat16)
        both_ref[slot, : used * BLK, :] = contract(kv, split, 1, 1)
        counts = jnp.where(pair_low, count_ref[blocks[0]], count_ref[blocks[1]])
        scores = [
            jnp.where(j < counts, both_ref[slot, j * BLK : (j + 1) * BLK, : 2 * BLK], jnp.float32(-1e30))
            for j in range(used)
        ]
        highest = jnp.max(folded(scores, jnp.maximum), axis=0, keepdims=True)
        expo = [jnp.exp(s - highest) for s in scores]
        inverse = 1.0 / jnp.sum(folded(expo, jnp.add), axis=0, keepdims=True)
        grads = [both_ref[slot, j * BLK : (j + 1) * BLK, 2 * BLK :] for j in range(used)]
        probs = [e * inverse for e in expo]
        delta = jnp.sum(folded([g * p for g, p in zip(grads, probs)], jnp.add), axis=0, keepdims=True)
        mixed = jnp.concatenate(
            [
                jnp.concatenate([(p * (g - delta)).astype(jnp.bfloat16), p.astype(jnp.bfloat16)], axis=1)
                for g, p in zip(grads, probs)
            ],
            axis=0,
        )
        crossed = contract(mixed, kv, 0, 0)
        for s, dq, o in (
            (starts[0], crossed[:64, :128], crossed[128:192, :128]),
            (starts[1], crossed[64:128, 128:], crossed[192:, 128:]),
        ):
            done_ref[pl.ds(s, BLK), : 2 * HD] = (dq * SCALE).astype(jnp.bfloat16)
            done_ref[pl.ds(s, BLK), 2 * HD :] = o.astype(jnp.bfloat16)
        return keys_at, contract(mixed, split, 1, 0)

    def grouped(used):
        def per_group(i, carry):
            found = [pair((i * PAIRS + u) * 2, u, used) for u in range(PAIRS)]
            for keys_at, parts in found:
                for c in range(2):
                    for j in range(used):
                        acc_ref[pl.ds(keys_at[c][j], BLK), :] += parts[
                            j * BLK : (j + 1) * BLK, c * 128 : (c + 1) * 128
                        ]
            return carry

        return per_group

    for step, used in enumerate(STEPS):
        lax.fori_loop(bounds_ref[step], bounds_ref[step + 1], grouped(used), 0)

    def assemble(t, carry):
        start = pl.multiple_of(t * TILE, TILE)
        turned = pltpu.roll(acc_ref[pl.ds(start, TILE), :], HD, 1).astype(jnp.bfloat16)
        rows = pl.ds(start, TILE)
        done_ref[rows, : 2 * HD] = jnp.where(low_lanes, done_ref[rows, : 2 * HD], turned)
        done_ref[rows, 2 * HD :] = jnp.where(low_lanes, turned, done_ref[rows, 2 * HD :])
        return carry

    lax.fori_loop(0, NODES // TILE, assemble, 0)
    row = lax.broadcasted_iota(jnp.int32, (128, NODES), 0).astype(jnp.float32).astype(jnp.bfloat16)
    full, empty = jnp.ones_like(row), jnp.zeros_like(row)

    def to_nodes(t, carry):
        start = pl.multiple_of(t * TILE, TILE)
        offsets = [
            jnp.clip(order_ref[...] - start - 128 * c, -1, 128).astype(jnp.float32).astype(jnp.bfloat16)
            for c in range(TILE // 128)
        ]
        pick = jnp.concatenate([jnp.where(row == offset, full, empty) for offset in offsets], axis=0)
        moved = contract(pick, done_ref[...], 1, 0)
        out_ref[pl.ds(start, TILE), :] = moved.astype(jnp.bfloat16)
        for c in range(TILE // ROWS):
            place = t * (TILE // ROWS) + c
            top, bottom = moved[c * ROWS : c * ROWS + HALF], moved[c * ROWS + HALF : (c + 1) * ROWS]
            late_top, late_bottom = top[:, 2 * HD :], bottom[:, 2 * HD :]
            attn_ref[place] = jnp.where(block_low, pltpu.roll(late_top, HD, 1), late_bottom).astype(jnp.bfloat16)
            grads_ref[place] = jnp.concatenate(
                [top[:, : 2 * HD], jnp.where(block_low, late_top, pltpu.roll(late_bottom, HD, 1)), bottom[:, : 2 * HD]],
                axis=1,
            ).astype(jnp.bfloat16)
        return carry

    lax.fori_loop(0, NODES // TILE, to_nodes, 0)


def ranking(counted):
    index = jnp.arange(NBLK)
    ahead = (counted[None, :] > counted[:, None]) | (
        (counted[None, :] == counted[:, None]) & (index[None, :] < index[:, None])
    )
    rank = jnp.sum(ahead.astype(jnp.int32), axis=1)
    ranked = jnp.sum(jnp.where(rank[None, :] == index[:, None], index[None, :], 0), axis=1)
    above = jnp.stack([jnp.sum((counted > limit).astype(jnp.int32)) for limit in STEPS[1:] + (0,)])
    group = 2 * PAIRS
    bounds = jnp.concatenate([jnp.zeros((1,), jnp.int32), (above + group - 1) // group])
    return ranked.astype(jnp.int32), bounds.astype(jnp.int32)


def attention(picked, counted, order, rows, after):
    ranked, bounds = ranking(counted)
    smem = pl.BlockSpec(memory_space=pltpu.SMEM)
    vmem = pl.BlockSpec(memory_space=pltpu.VMEM)
    return pl.pallas_call(
        attention_kernel,
        out_shape=(
            jax.ShapeDtypeStruct((NODES, WIDE), jnp.bfloat16),
            jax.ShapeDtypeStruct((SEQ, HALF, 2 * HD), jnp.bfloat16),
            jax.ShapeDtypeStruct((SEQ, HALF, 6 * HD), jnp.bfloat16),
        ),
        in_specs=[smem, smem, smem, smem, vmem, vmem, pl.BlockSpec(memory_space=pl.ANY)],
        out_specs=(vmem, vmem, vmem),
        scratch_shapes=[
            pltpu.VMEM((NODES, 2 * HD), jnp.bfloat16),
            pltpu.VMEM((NODES, 2 * HD), jnp.bfloat16),
            pltpu.VMEM((NODES, 2 * HD), jnp.float32),
            pltpu.VMEM((NODES, WIDE), jnp.bfloat16),
            pltpu.VMEM((PAIRS, MAXB * BLK, 4 * BLK), jnp.float32),
        ],
        compiler_params=pltpu.CompilerParams(vmem_limit_bytes=VMEM_BYTES),
        cost_estimate=pl.CostEstimate(flops=10_000_000_000, bytes_accessed=4_000_000, transcendentals=1_000_000),
        name="clustered_attention",
    )(picked, counted, ranked, bounds, order, rows, after)


def project_kernel(features_ref, upstream_ref, w_qkv_ref, w_out_ref, sent_ref, normed_ref):
    @pl.when(pl.program_id(0) == 0)
    def _():
        wide = features_ref[...].astype(jnp.float32)
        inv_rms = lax.rsqrt(jnp.mean(wide * wide, axis=-1, keepdims=True) + EPS)
        normed_ref[...] = (wide * inv_rms).astype(jnp.bfloat16)

    packed = contract(normed_ref[...], w_qkv_ref[...], 1, 0)
    grads = contract(upstream_ref[...], w_out_ref[...], 1, 1)
    for k in range(2):
        sent_ref[k] = jnp.concatenate(
            [packed[:, k * 3 * HD : (k + 1) * 3 * HD], grads[:, k * HD : (k + 1) * HD]], axis=1
        ).astype(jnp.bfloat16)


def project(features, upstream, w_qkv, w_out):
    whole = pl.BlockSpec((ROWS, D), lambda i: (0, 0))
    return pl.pallas_call(
        project_kernel,
        grid=(H // 2,),
        out_shape=(
            jax.ShapeDtypeStruct((H, ROWS, WIDE), jnp.bfloat16),
            jax.ShapeDtypeStruct((ROWS, D), jnp.bfloat16),
        ),
        in_specs=[
            whole,
            whole,
            pl.BlockSpec((D, 6 * HD), lambda i: (0, i)),
            pl.BlockSpec((2 * HD, D), lambda i: (i, 0)),
        ],
        out_specs=(pl.BlockSpec((2, ROWS, WIDE), lambda i: (i, 0, 0)), whole),
        compiler_params=pltpu.CompilerParams(vmem_limit_bytes=VMEM_BYTES),
        cost_estimate=pl.CostEstimate(flops=2 * ROWS * D * 4 * D, bytes_accessed=9_500_000, transcendentals=ROWS),
        name="project",
    )(features, upstream, w_qkv, w_out)


def node_rows(one, two):
    halves = [jnp.concatenate([one[:, lanes], two[:, lanes]], axis=1) for lanes in (slice(0, HD), slice(HD, 2 * HD))]
    return jnp.concatenate(halves, axis=0)


def finish_kernel(features_ref, upstream_ref, attn_ref, grads_ref, w_qkv_ref, w_out_ref, mixed_ref, grad_ref, mixed_acc, grad_acc):
    step = pl.program_id(0)

    @pl.when(step == 0)
    def _():
        mixed_acc[...] = features_ref[...].astype(jnp.float32)
        grad_acc[...] = jnp.zeros_like(grad_acc)

    attn, grads = node_rows(attn_ref[0], attn_ref[1]), []
    for k in range(2):
        block = grads_ref[k]
        first, values, second = block[:, : 2 * HD], block[:, 2 * HD : 4 * HD], block[:, 4 * HD :]
        grads.append(
            jnp.concatenate(
                [
                    jnp.concatenate([first, values[:, :HD]], axis=1),
                    jnp.concatenate([second, values[:, HD:]], axis=1),
                ],
                axis=0,
            )
        )
    grads = jnp.concatenate(grads, axis=1)
    mixed_acc[...] += contract(attn, w_out_ref[...], 1, 0)
    grad_acc[...] += contract(grads, w_qkv_ref[...], 1, 1)

    @pl.when(step == pl.num_programs(0) - 1)
    def _():
        wide = features_ref[...].astype(jnp.float32)
        inv_rms = lax.rsqrt(jnp.mean(wide * wide, axis=-1, keepdims=True) + EPS)
        grad_normed = grad_acc[...]
        inner = jnp.mean(grad_normed * wide, axis=-1, keepdims=True)
        mixed_ref[...] = mixed_acc[...].astype(jnp.bfloat16)
        grad_ref[...] = (
            upstream_ref[...].astype(jnp.float32)
            + inv_rms * grad_normed
            - wide * inv_rms * inv_rms * inv_rms * inner
        ).astype(jnp.bfloat16)


def finish(features, upstream, attn, grads, w_qkv, w_out):
    whole = pl.BlockSpec((ROWS, D), lambda i: (0, 0))
    return pl.pallas_call(
        finish_kernel,
        grid=(H // 2,),
        out_shape=(jax.ShapeDtypeStruct((ROWS, D), jnp.bfloat16),) * 2,
        in_specs=[
            whole,
            whole,
            pl.BlockSpec((2, HALF, 2 * HD), lambda i: (i, 0, 0)),
            pl.BlockSpec((2, HALF, 6 * HD), lambda i: (i, 0, 0)),
            pl.BlockSpec((D, 6 * HD), lambda i: (0, i)),
            pl.BlockSpec((2 * HD, D), lambda i: (i, 0)),
        ],
        out_specs=(whole, whole),
        scratch_shapes=[pltpu.VMEM((ROWS, D), jnp.float32)] * 2,
        compiler_params=pltpu.CompilerParams(vmem_limit_bytes=VMEM_BYTES),
        cost_estimate=pl.CostEstimate(flops=2 * ROWS * D * 4 * D, bytes_accessed=10_000_000, transcendentals=ROWS),
        name="finish",
    )(features, upstream, attn, grads, w_qkv, w_out)


CORES = 2
CHIPS = DP // CORES
SHARE = ROWS + 3 * HD


def place():
    me = lax.axis_index("dp")
    return me // CORES, me % CORES


def stacked(blocks, after):
    def kernel(*refs):
        for k in range(len(blocks)):
            refs[-1][k * ROWS : (k + 1) * ROWS] = refs[k][...]

    vmem = pl.BlockSpec(memory_space=pltpu.VMEM)
    return pl.pallas_call(
        kernel,
        out_shape=jax.ShapeDtypeStruct((len(blocks) * ROWS, D), jnp.bfloat16),
        in_specs=[vmem] * len(blocks) + [pl.BlockSpec(memory_space=pl.ANY)],
        out_specs=vmem,
        compiler_params=pltpu.CompilerParams(vmem_limit_bytes=VMEM_BYTES),
        cost_estimate=pl.CostEstimate(flops=0, bytes_accessed=4 * D * ROWS * len(blocks), transcendentals=0),
        name="stacked",
    )(*blocks, after)


def weight_qkv_kernel(out_ref, nodes_ref, sent_ref):
    total = None
    for t in range(NODES // CHUNK):
        rows = slice(t * CHUNK, (t + 1) * CHUNK)
        wide = nodes_ref[rows, :].astype(jnp.float32)
        inv_rms = lax.rsqrt(jnp.mean(wide * wide, axis=-1, keepdims=True) + EPS)
        part = contract(out_ref[rows, : 3 * HD], (wide * inv_rms).astype(jnp.bfloat16), 0, 0)
        total = part if total is None else total + part
    for i in range(DP):
        sent_ref[i] = total[:, i * ROWS : (i + 1) * ROWS].astype(jnp.bfloat16)


def weight_qkv(head_out, all_nodes):
    vmem = pl.BlockSpec(memory_space=pltpu.VMEM)
    return pl.pallas_call(
        weight_qkv_kernel,
        out_shape=jax.ShapeDtypeStruct((DP, 3 * HD, ROWS), jnp.bfloat16),
        in_specs=[vmem, vmem],
        out_specs=vmem,
        compiler_params=pltpu.CompilerParams(vmem_limit_bytes=VMEM_BYTES),
        cost_estimate=pl.CostEstimate(flops=2 * NODES * D * 3 * HD, bytes_accessed=6_000_000, transcendentals=0),
        name="weight_qkv",
    )(head_out, all_nodes)


def shares_kernel(attn_ref, qkv_ref, grads_ref, own_ref, sent_ref, through_ref):
    _, core = place()
    for chip in range(CHIPS):
        for ref, c in ((own_ref, core), (sent_ref, 1 - core)):
            i = chip * CORES + c
            ref[chip, :HALF] = attn_ref[2 * i]
            ref[chip, HALF:ROWS] = attn_ref[2 * i + 1]
            ref[chip, ROWS:] = qkv_ref[i]


def shares(attn, part_qkv, grads):
    vmem = pl.BlockSpec(memory_space=pltpu.VMEM)
    anywhere = pl.BlockSpec(memory_space=pl.ANY)
    share = jax.ShapeDtypeStruct((CHIPS, SHARE, ROWS), jnp.bfloat16)
    return pl.pallas_call(
        shares_kernel,
        out_shape=(share, share, jax.ShapeDtypeStruct(grads.shape, grads.dtype)),
        in_specs=[vmem, vmem, anywhere],
        out_specs=(vmem, vmem, anywhere),
        input_output_aliases={2: 2},
        compiler_params=pltpu.CompilerParams(vmem_limit_bytes=VMEM_BYTES),
        name="shares",
    )(attn, part_qkv, grads)


def chips_kernel(own_ref, other_ref, *sent_refs):
    y, core = place()
    for step, ref in enumerate(sent_refs):
        chip = (y + step) % CHIPS
        own, other = own_ref[chip], other_ref[chip]
        first = core == 0
        ref[:ROWS] = jnp.where(first, own[:ROWS], other[:ROWS])
        ref[ROWS : 2 * ROWS] = jnp.where(first, other[:ROWS], own[:ROWS])
        ref[2 * ROWS :] = (own[ROWS:].astype(jnp.float32) + other[ROWS:].astype(jnp.float32)).astype(jnp.bfloat16)


def over_dp(own, sent):
    other = lax.ppermute(sent, "dp", [(i, i ^ 1) for i in range(DP)])
    vmem = pl.BlockSpec(memory_space=pltpu.VMEM)
    shape = jax.ShapeDtypeStruct((ROWS + SHARE, ROWS), jnp.bfloat16)
    parts = pl.pallas_call(
        chips_kernel,
        out_shape=(shape,) * CHIPS,
        in_specs=[vmem, vmem],
        out_specs=(vmem,) * CHIPS,
        compiler_params=pltpu.CompilerParams(vmem_limit_bytes=VMEM_BYTES),
        name="chips",
    )(own, other)
    return parts[0], *(lax.ppermute(parts[step], "dp", chip_shift(step)) for step in (1, 2, 3))


def chip_shift(step):
    return [(i, (i + step * CORES) % DP) for i in range(DP)]


def batches_of(block, after):
    moved = [lax.ppermute(block, "dp", chip_shift(step)) for step in (1, 2, 3)]
    mine = stacked((block, *moved), after)
    return mine, lax.ppermute(mine, "dp", [(i, i ^ 1) for i in range(DP)])


def weight_out_kernel(*refs):
    parts, (mine_ref, other_ref, sent_ref) = refs[:CHIPS], refs[CHIPS:]
    _, core = place()
    total, mine, other = None, [], []
    for ref in parts:
        qkv = ref[2 * ROWS :].astype(jnp.float32)
        total = qkv if total is None else total + qkv
        attn = [node_rows(ref[c * ROWS : c * ROWS + HALF], ref[c * ROWS + HALF : (c + 1) * ROWS]) for c in range(CORES)]
        mine.append(jnp.where(core == 0, attn[0], attn[1]))
        other.append(jnp.where(core == 0, attn[1], attn[0]))
    out = contract(jnp.concatenate(mine, axis=0), mine_ref[...], 0, 0)
    out += contract(jnp.concatenate(other, axis=0), other_ref[...], 0, 0)
    qkv = jnp.transpose(total)
    nothing = jnp.zeros((8, HD), jnp.float32)
    for s in range(SEQ):
        rows = slice(s * 8, (s + 1) * 8)
        sent_ref[s] = jnp.concatenate(
            [
                jnp.concatenate([out[rows, : D // 2], out[rows, D // 2 :]], axis=0),
                jnp.concatenate(
                    [qkv[rows, : 2 * HD], jnp.concatenate([qkv[rows, 2 * HD :], nothing], axis=1)], axis=0
                ),
            ],
            axis=1,
        ).astype(jnp.bfloat16)


def weight_out(parts, mine, other):
    vmem = pl.BlockSpec(memory_space=pltpu.VMEM)
    return pl.pallas_call(
        weight_out_kernel,
        out_shape=jax.ShapeDtypeStruct((SEQ, 16, D // 2 + 2 * HD), jnp.bfloat16),
        in_specs=[vmem] * (CHIPS + 2),
        out_specs=vmem,
        compiler_params=pltpu.CompilerParams(vmem_limit_bytes=VMEM_BYTES),
        cost_estimate=pl.CostEstimate(flops=2 * DP * ROWS * D * ROWS, bytes_accessed=3_000_000, transcendentals=0),
        name="weight_out",
    )(*parts, mine, other)


def fold_kernel(parts_ref, qkv_ref, out_ref):
    total = parts_ref[0, :, : D // 2].astype(jnp.float32)
    for s in range(1, SEQ):
        total = total + parts_ref[s, :, : D // 2].astype(jnp.float32)
    out_ref[:, : D // 2] = total[:8]
    out_ref[:, D // 2 :] = total[8:]
    for h in range(H):
        part = parts_ref[h, :, D // 2 :].astype(jnp.float32)
        qkv_ref[:, h * 3 * HD : (h + 1) * 3 * HD] = jnp.concatenate([part[:8], part[8:, :HD]], axis=1)


def fold(parts):
    vmem = pl.BlockSpec(memory_space=pltpu.VMEM)
    return pl.pallas_call(
        fold_kernel,
        out_shape=(
            jax.ShapeDtypeStruct((8, 3 * D), jnp.float32),
            jax.ShapeDtypeStruct((8, D), jnp.float32),
        ),
        in_specs=[vmem],
        out_specs=(vmem, vmem),
        name="fold",
    )(parts)


def shards(nodes, w_qkv, w_out, cotangent, order, block_list, block_count):
    features, upstream = nodes[0], cotangent[0]
    all_nodes = lax.all_gather(features, "seq", axis=0, tiled=True)
    sent, _ = project(features, upstream, w_qkv, w_out)
    head_rows = lax.all_to_all(sent, "seq", 0, 0, tiled=True).reshape(NODES, WIDE)
    upstreams = batches_of(upstream, sent)
    head_out, attn_sent, grads_sent = attention(block_list[0], block_count[0], order, head_rows, upstreams[0])
    attn = lax.all_to_all(attn_sent, "seq", 0, 0, tiled=True)

    own, sent, grads_sent = shares(attn, weight_qkv(head_out, all_nodes), grads_sent)
    grads = lax.all_to_all(grads_sent, "seq", 0, 0, tiled=True)
    parts = weight_out(over_dp(own, sent), *upstreams)
    grad_qkv, grad_out = fold(lax.all_to_all(parts, "seq", 0, 0, tiled=True))

    mixed, grad_nodes = finish(features, upstream, attn, grads, w_qkv, w_out)
    return mixed[None], grad_nodes[None], grad_qkv, grad_out


def solution(mesh):
    return jax.shard_map(
        shards,
        mesh=mesh,
        in_specs=(
            P("dp", "seq", None),
            P(),
            P(),
            P("dp", "seq", None),
            P("dp", None),
            P("dp", None, None),
            P("dp", None),
        ),
        out_specs=(
            P("dp", "seq", None),
            P("dp", "seq", None),
            P(("dp", "seq"), None),
            P(("dp", "seq"), None),
        ),
        check_vma=False,
    )
```

```python
import math

import jax
import jax.numpy as jnp
from jax import lax
from jax.experimental import pallas as pl
from jax.experimental.pallas import tpu as pltpu
from jax.sharding import PartitionSpec as P

H = 16
HD = 64
D = 1024
BLK = 64
MAXB = 8
NODES = 2048
NBLK = 32
WIDE = 4 * HD
TILE = 2048
PAIRS = 2
STEPS = (8, 4)
DP = 8
SEQ = 16
ROWS = 128
CHUNK = 512
HALF = ROWS // 2
STEP = 8
FEW = 2
VMEM_BYTES = 60 * 1024 * 1024
EPS = 1e-05
SCALE = 1.0 / math.sqrt(HD)


def contract(a, b, da, db):
    return lax.dot_general(a, b, (((da,), (db,)), ((), ())), preferred_element_type=jnp.float32)


def attention_kernel(
    list_ref, count_ref, ranked_ref, bounds_ref, order_ref, rows_ref, after_ref, out_ref, attn_ref, grads_ref, qg_ref, kv_ref, acc_ref, done_ref, both_ref
):
    low_lanes = lax.broadcasted_iota(jnp.int32, (TILE, 2 * HD), 1) < HD
    one, none = jnp.ones((TILE, 128), jnp.bfloat16), jnp.zeros((TILE, 128), jnp.bfloat16)

    def to_cluster(t, carry):
        start = pl.multiple_of(t * TILE, TILE)
        ordered = jnp.broadcast_to(order_ref[:, pl.ds(start, TILE)], (128, TILE))
        position = jnp.transpose(ordered.astype(jnp.float32)).astype(jnp.int32)
        lanes = lax.broadcasted_iota(jnp.int32, (TILE, 128), 1)
        within = (position % 128 == lanes).astype(jnp.float32).astype(jnp.bfloat16)
        tile_of = (position // 128).astype(jnp.float32).astype(jnp.bfloat16)
        pick = jnp.concatenate(
            [jnp.where(tile_of == jnp.bfloat16(c), within, none) for c in range(NODES // 128)], axis=1
        )
        moved = contract(pick, rows_ref[...], 1, 0)
        first, second = moved[:, : 2 * HD], moved[:, 2 * HD :]
        qg_ref[pl.ds(start, TILE), :] = jnp.where(low_lanes, first * SCALE, second).astype(jnp.bfloat16)
        kv_ref[pl.ds(start, TILE), :] = jnp.where(
            low_lanes, pltpu.roll(first, HD, 1), pltpu.roll(second, HD, 1)
        ).astype(jnp.bfloat16)
        return carry

    lax.fori_loop(0, NODES // TILE, to_cluster, 0)
    acc_ref[...] = jnp.zeros_like(acc_ref)
    block_low = lax.broadcasted_iota(jnp.int32, (BLK, 2 * HD), 1) < HD
    pair_low = lax.broadcasted_iota(jnp.int32, (1, 2 * BLK), 1) < BLK

    def folded(parts, op):
        total = parts[0]
        for part in parts[1:]:
            total = op(total, part)
        return total

    def pair(at, slot, used):
        blocks = (ranked_ref[at], ranked_ref[at + 1])
        starts = [pl.multiple_of(b * BLK, BLK) for b in blocks]
        qg = [qg_ref[pl.ds(s, BLK), :].astype(jnp.float32) for s in starts]
        keys_at = [[pl.multiple_of(list_ref[b, j] * BLK, BLK) for j in range(used)] for b in blocks]
        kv = jnp.concatenate(
            [jnp.concatenate([kv_ref[pl.ds(key, BLK), :] for key in keys], axis=0) for keys in keys_at], axis=1
        )
        zero = jnp.zeros_like(qg[0])
        q0, q1 = (jnp.where(block_low, x, zero) for x in qg)
        g0, g1 = (jnp.where(block_low, zero, x) for x in qg)
        split = jnp.concatenate(
            [
                jnp.concatenate([q0, zero, g0, zero], axis=0),
                jnp.concatenate([zero, q1, zero, g1], axis=0),
            ],
            axis=1,
        ).astype(jnp.bfloat16)
        both_ref[slot, : used * BLK, :] = contract(kv, split, 1, 1)
        counts = jnp.where(pair_low, count_ref[blocks[0]], count_ref[blocks[1]])
        scores = [
            jnp.where(j < counts, both_ref[slot, j * BLK : (j + 1) * BLK, : 2 * BLK], jnp.float32(-1e30))
            for j in range(used)
        ]
        highest = jnp.max(folded(scores, jnp.maximum), axis=0, keepdims=True)
        expo = [jnp.exp(s - highest) for s in scores]
        inverse = 1.0 / jnp.sum(folded(expo, jnp.add), axis=0, keepdims=True)
        grads = [both_ref[slot, j * BLK : (j + 1) * BLK, 2 * BLK :] for j in range(used)]
        probs = [e * inverse for e in expo]
        delta = jnp.sum(folded([g * p for g, p in zip(grads, probs)], jnp.add), axis=0, keepdims=True)
        mixed = jnp.concatenate(
            [
                jnp.concatenate([(p * (g - delta)).astype(jnp.bfloat16), p.astype(jnp.bfloat16)], axis=1)
                for g, p in zip(grads, probs)
            ],
            axis=0,
        )
        crossed = contract(mixed, kv, 0, 0)
        for s, dq, o in (
            (starts[0], crossed[:64, :128], crossed[128:192, :128]),
            (starts[1], crossed[64:128, 128:], crossed[192:, 128:]),
        ):
            done_ref[pl.ds(s, BLK), : 2 * HD] = (dq * SCALE).astype(jnp.bfloat16)
            done_ref[pl.ds(s, BLK), 2 * HD :] = o.astype(jnp.bfloat16)
        return keys_at, contract(mixed, split, 1, 0)

    def grouped(used):
        def per_group(i, carry):
            found = [pair((i * PAIRS + u) * 2, u, used) for u in range(PAIRS)]
            for keys_at, parts in found:
                for c in range(2):
                    for j in range(used):
                        acc_ref[pl.ds(keys_at[c][j], BLK), :] += parts[
                            j * BLK : (j + 1) * BLK, c * 128 : (c + 1) * 128
                        ]
            return carry

        return per_group

    for step, used in enumerate(STEPS):
        lax.fori_loop(bounds_ref[step], bounds_ref[step + 1], grouped(used), 0)

    def assemble(t, carry):
        start = pl.multiple_of(t * TILE, TILE)
        turned = pltpu.roll(acc_ref[pl.ds(start, TILE), :], HD, 1).astype(jnp.bfloat16)
        rows = pl.ds(start, TILE)
        done_ref[rows, : 2 * HD] = jnp.where(low_lanes, done_ref[rows, : 2 * HD], turned)
        done_ref[rows, 2 * HD :] = jnp.where(low_lanes, turned, done_ref[rows, 2 * HD :])
        return carry

    lax.fori_loop(0, NODES // TILE, assemble, 0)
    row = lax.broadcasted_iota(jnp.int32, (128, NODES), 0).astype(jnp.float32).astype(jnp.bfloat16)
    full, empty = jnp.ones_like(row), jnp.zeros_like(row)

    def to_nodes(t, carry):
        start = pl.multiple_of(t * TILE, TILE)
        offsets = [
            jnp.clip(order_ref[...] - start - 128 * c, -1, 128).astype(jnp.float32).astype(jnp.bfloat16)
            for c in range(TILE // 128)
        ]
        pick = jnp.concatenate([jnp.where(row == offset, full, empty) for offset in offsets], axis=0)
        moved = contract(pick, done_ref[...], 1, 0)
        out_ref[pl.ds(start, TILE), :] = moved.astype(jnp.bfloat16)
        for c in range(TILE // ROWS):
            place = t * (TILE // ROWS) + c
            top, bottom = moved[c * ROWS : c * ROWS + HALF], moved[c * ROWS + HALF : (c + 1) * ROWS]
            late_top, late_bottom = top[:, 2 * HD :], bottom[:, 2 * HD :]
            attn_ref[place] = jnp.where(block_low, pltpu.roll(late_top, HD, 1), late_bottom).astype(jnp.bfloat16)
            grads_ref[place] = jnp.concatenate(
                [top[:, : 2 * HD], jnp.where(block_low, late_top, pltpu.roll(late_bottom, HD, 1)), bottom[:, : 2 * HD]],
                axis=1,
            ).astype(jnp.bfloat16)
        return carry

    lax.fori_loop(0, NODES // TILE, to_nodes, 0)


def ranking(counted):
    index = jnp.arange(NBLK)
    ahead = (counted[None, :] > counted[:, None]) | (
        (counted[None, :] == counted[:, None]) & (index[None, :] < index[:, None])
    )
    rank = jnp.sum(ahead.astype(jnp.int32), axis=1)
    ranked = jnp.sum(jnp.where(rank[None, :] == index[:, None], index[None, :], 0), axis=1)
    above = jnp.stack([jnp.sum((counted > limit).astype(jnp.int32)) for limit in STEPS[1:] + (0,)])
    group = 2 * PAIRS
    bounds = jnp.concatenate([jnp.zeros((1,), jnp.int32), (above + group - 1) // group])
    return ranked.astype(jnp.int32), bounds.astype(jnp.int32)


def attention(picked, counted, order, rows, after):
    ranked, bounds = ranking(counted)
    smem = pl.BlockSpec(memory_space=pltpu.SMEM)
    vmem = pl.BlockSpec(memory_space=pltpu.VMEM)
    return pl.pallas_call(
        attention_kernel,
        out_shape=(
            jax.ShapeDtypeStruct((NODES, WIDE), jnp.bfloat16),
            jax.ShapeDtypeStruct((SEQ, HALF, 2 * HD), jnp.bfloat16),
            jax.ShapeDtypeStruct((SEQ, HALF, 6 * HD), jnp.bfloat16),
        ),
        in_specs=[smem, smem, smem, smem, vmem, vmem, pl.BlockSpec(memory_space=pl.ANY)],
        out_specs=(vmem, vmem, vmem),
        scratch_shapes=[
            pltpu.VMEM((NODES, 2 * HD), jnp.bfloat16),
            pltpu.VMEM((NODES, 2 * HD), jnp.bfloat16),
            pltpu.VMEM((NODES, 2 * HD), jnp.float32),
            pltpu.VMEM((NODES, WIDE), jnp.bfloat16),
            pltpu.VMEM((PAIRS, MAXB * BLK, 4 * BLK), jnp.float32),
        ],
        compiler_params=pltpu.CompilerParams(vmem_limit_bytes=VMEM_BYTES),
        cost_estimate=pl.CostEstimate(flops=10_000_000_000, bytes_accessed=4_000_000, transcendentals=1_000_000),
        name="clustered_attention",
    )(picked, counted, ranked, bounds, order, rows, after)


def project_kernel(features_ref, upstream_ref, w_qkv_ref, w_out_ref, sent_ref, normed_ref):
    @pl.when(pl.program_id(0) == 0)
    def _():
        wide = features_ref[...].astype(jnp.float32)
        inv_rms = lax.rsqrt(jnp.mean(wide * wide, axis=-1, keepdims=True) + EPS)
        normed_ref[...] = (wide * inv_rms).astype(jnp.bfloat16)

    packed = contract(normed_ref[...], w_qkv_ref[...], 1, 0)
    grads = contract(upstream_ref[...], w_out_ref[...], 1, 1)
    for k in range(FEW):
        sent_ref[k] = jnp.concatenate(
            [packed[:, k * 3 * HD : (k + 1) * 3 * HD], grads[:, k * HD : (k + 1) * HD]], axis=1
        ).astype(jnp.bfloat16)


def project(features, upstream, w_qkv, w_out):
    whole = pl.BlockSpec((ROWS, D), lambda i: (0, 0))
    return pl.pallas_call(
        project_kernel,
        grid=(H // FEW,),
        out_shape=(
            jax.ShapeDtypeStruct((H, ROWS, WIDE), jnp.bfloat16),
            jax.ShapeDtypeStruct((ROWS, D), jnp.bfloat16),
        ),
        in_specs=[
            whole,
            whole,
            pl.BlockSpec((D, 3 * FEW * HD), lambda i: (0, i)),
            pl.BlockSpec((FEW * HD, D), lambda i: (i, 0)),
        ],
        out_specs=(pl.BlockSpec((FEW, ROWS, WIDE), lambda i: (i, 0, 0)), whole),
        compiler_params=pltpu.CompilerParams(vmem_limit_bytes=VMEM_BYTES),
        cost_estimate=pl.CostEstimate(flops=2 * ROWS * D * 4 * D, bytes_accessed=9_500_000, transcendentals=ROWS),
        name="project",
    )(features, upstream, w_qkv, w_out)


def node_rows(*heads):
    halves = [jnp.concatenate([h[:, lanes] for h in heads], axis=1) for lanes in (slice(0, HD), slice(HD, 2 * HD))]
    return jnp.concatenate(halves, axis=0)


def finish_kernel(features_ref, upstream_ref, attn_ref, grads_ref, w_qkv_ref, w_out_ref, mixed_ref, grad_ref, mixed_acc, grad_acc):
    step = pl.program_id(0)

    @pl.when(step == 0)
    def _():
        mixed_acc[...] = features_ref[...].astype(jnp.float32)
        grad_acc[...] = jnp.zeros_like(grad_acc)

    attn = node_rows(*(attn_ref[k] for k in range(STEP)))
    first, second = [], []
    for k in range(STEP):
        block = grads_ref[k]
        first += [block[:, : 2 * HD], block[:, 2 * HD : 3 * HD]]
        second += [block[:, 4 * HD :], block[:, 3 * HD : 4 * HD]]
    grads = jnp.concatenate([jnp.concatenate(first, axis=1), jnp.concatenate(second, axis=1)], axis=0)
    mixed_acc[...] += contract(attn, w_out_ref[...], 1, 0)
    grad_acc[...] += contract(grads, w_qkv_ref[...], 1, 1)

    @pl.when(step == pl.num_programs(0) - 1)
    def _():
        wide = features_ref[...].astype(jnp.float32)
        inv_rms = lax.rsqrt(jnp.mean(wide * wide, axis=-1, keepdims=True) + EPS)
        grad_normed = grad_acc[...]
        inner = jnp.mean(grad_normed * wide, axis=-1, keepdims=True)
        mixed_ref[...] = mixed_acc[...].astype(jnp.bfloat16)
        grad_ref[...] = (
            upstream_ref[...].astype(jnp.float32)
            + inv_rms * grad_normed
            - wide * inv_rms * inv_rms * inv_rms * inner
        ).astype(jnp.bfloat16)


def finish(features, upstream, attn, grads, w_qkv, w_out):
    whole = pl.BlockSpec((ROWS, D), lambda i: (0, 0))
    return pl.pallas_call(
        finish_kernel,
        grid=(H // STEP,),
        out_shape=(jax.ShapeDtypeStruct((ROWS, D), jnp.bfloat16),) * 2,
        in_specs=[
            whole,
            whole,
            pl.BlockSpec((STEP, HALF, 2 * HD), lambda i: (i, 0, 0)),
            pl.BlockSpec((STEP, HALF, 6 * HD), lambda i: (i, 0, 0)),
            pl.BlockSpec((D, 3 * STEP * HD), lambda i: (0, i)),
            pl.BlockSpec((STEP * HD, D), lambda i: (i, 0)),
        ],
        out_specs=(whole, whole),
        scratch_shapes=[pltpu.VMEM((ROWS, D), jnp.float32)] * 2,
        compiler_params=pltpu.CompilerParams(vmem_limit_bytes=VMEM_BYTES),
        cost_estimate=pl.CostEstimate(flops=2 * ROWS * D * 4 * D, bytes_accessed=10_000_000, transcendentals=ROWS),
        name="finish",
    )(features, upstream, attn, grads, w_qkv, w_out)


CORES = 2
CHIPS = DP // CORES


def stacked(blocks, after):
    def kernel(*refs):
        for k in range(len(blocks)):
            refs[-1][k * ROWS : (k + 1) * ROWS] = refs[k][...]

    vmem = pl.BlockSpec(memory_space=pltpu.VMEM)
    return pl.pallas_call(
        kernel,
        out_shape=jax.ShapeDtypeStruct((len(blocks) * ROWS, D), jnp.bfloat16),
        in_specs=[vmem] * len(blocks) + [pl.BlockSpec(memory_space=pl.ANY)],
        out_specs=vmem,
        compiler_params=pltpu.CompilerParams(vmem_limit_bytes=VMEM_BYTES),
        cost_estimate=pl.CostEstimate(flops=0, bytes_accessed=4 * D * ROWS * len(blocks), transcendentals=0),
        name="stacked",
    )(*blocks, after)


def weight_qkv_kernel(out_ref, nodes_ref, grads_ref, sent_ref, through_ref):
    total = None
    for t in range(NODES // CHUNK):
        rows = slice(t * CHUNK, (t + 1) * CHUNK)
        wide = nodes_ref[rows, :].astype(jnp.float32)
        inv_rms = lax.rsqrt(jnp.mean(wide * wide, axis=-1, keepdims=True) + EPS)
        part = contract(out_ref[rows, : 3 * HD], (wide * inv_rms).astype(jnp.bfloat16), 0, 0)
        total = part if total is None else total + part
    for i in range(DP):
        sent_ref[i] = total[:, i * ROWS : (i + 1) * ROWS].astype(jnp.bfloat16)


def weight_qkv(head_out, all_nodes, grads):
    vmem = pl.BlockSpec(memory_space=pltpu.VMEM)
    anywhere = pl.BlockSpec(memory_space=pl.ANY)
    return pl.pallas_call(
        weight_qkv_kernel,
        out_shape=(
            jax.ShapeDtypeStruct((DP, 3 * HD, ROWS), jnp.bfloat16),
            jax.ShapeDtypeStruct(grads.shape, grads.dtype),
        ),
        in_specs=[vmem, vmem, anywhere],
        out_specs=(vmem, anywhere),
        input_output_aliases={2: 1},
        compiler_params=pltpu.CompilerParams(vmem_limit_bytes=VMEM_BYTES),
        cost_estimate=pl.CostEstimate(flops=2 * NODES * D * 3 * HD, bytes_accessed=6_000_000, transcendentals=0),
        name="weight_qkv",
    )(head_out, all_nodes, grads)


def chips_kernel(attn_ref, qkv_ref, other_attn_ref, other_qkv_ref, *sent_refs):
    me = lax.axis_index("dp")
    y, core = me // CORES, me % CORES
    first = core == 0
    for step, ref in enumerate(sent_refs):
        i = ((y + step) % CHIPS) * CORES + core
        for k in range(2):
            own, other = attn_ref[2 * i + k], other_attn_ref[2 * i + k]
            ref[k * HALF : (k + 1) * HALF] = jnp.where(first, own, other)
            ref[ROWS + k * HALF : ROWS + (k + 1) * HALF] = jnp.where(first, other, own)
        total = qkv_ref[i].astype(jnp.float32) + other_qkv_ref[i].astype(jnp.float32)
        ref[2 * ROWS :] = total.astype(jnp.bfloat16)


def over_dp(attn, part_qkv):
    pairs = [(i, i ^ 1) for i in range(DP)]
    vmem = pl.BlockSpec(memory_space=pltpu.VMEM)
    shape = jax.ShapeDtypeStruct((2 * ROWS + 3 * HD, ROWS), jnp.bfloat16)
    parts = pl.pallas_call(
        chips_kernel,
        out_shape=(shape,) * CHIPS,
        in_specs=[vmem] * 4,
        out_specs=(vmem,) * CHIPS,
        compiler_params=pltpu.CompilerParams(vmem_limit_bytes=VMEM_BYTES),
        cost_estimate=pl.CostEstimate(flops=0, bytes_accessed=2_000_000, transcendentals=0),
        name="chips",
    )(attn, part_qkv, lax.ppermute(attn, "dp", pairs), lax.ppermute(part_qkv, "dp", pairs))
    return parts[0], *(lax.ppermute(parts[step], "dp", chip_shift(step)) for step in (1, 2, 3))


def chip_shift(step):
    return [(i, (i + step * CORES) % DP) for i in range(DP)]


def batches_of(block, after):
    moved = [lax.ppermute(block, "dp", chip_shift(step)) for step in (1, 2, 3)]
    mine = stacked((block, *moved), after)
    return mine, lax.ppermute(mine, "dp", [(i, i ^ 1) for i in range(DP)])


def weight_out_kernel(*refs):
    parts, (mine_ref, other_ref, sent_ref) = refs[:CHIPS], refs[CHIPS:]
    core = lax.axis_index("dp") % CORES
    total, mine, other = None, [], []
    for ref in parts:
        qkv = ref[2 * ROWS :].astype(jnp.float32)
        total = qkv if total is None else total + qkv
        attn = [node_rows(ref[c * ROWS : c * ROWS + HALF], ref[c * ROWS + HALF : (c + 1) * ROWS]) for c in range(CORES)]
        mine.append(jnp.where(core == 0, attn[0], attn[1]))
        other.append(jnp.where(core == 0, attn[1], attn[0]))
    out = contract(jnp.concatenate(mine, axis=0), mine_ref[...], 0, 0)
    out += contract(jnp.concatenate(other, axis=0), other_ref[...], 0, 0)
    qkv = jnp.transpose(total)
    nothing = jnp.zeros((8, HD), jnp.float32)
    for s in range(SEQ):
        rows = slice(s * 8, (s + 1) * 8)
        sent_ref[s] = jnp.concatenate(
            [
                jnp.concatenate([out[rows, : D // 2], out[rows, D // 2 :]], axis=0),
                jnp.concatenate(
                    [qkv[rows, : 2 * HD], jnp.concatenate([qkv[rows, 2 * HD :], nothing], axis=1)], axis=0
                ),
            ],
            axis=1,
        ).astype(jnp.bfloat16)


def weight_out(parts, mine, other):
    vmem = pl.BlockSpec(memory_space=pltpu.VMEM)
    return pl.pallas_call(
        weight_out_kernel,
        out_shape=jax.ShapeDtypeStruct((SEQ, 16, D // 2 + 2 * HD), jnp.bfloat16),
        in_specs=[vmem] * (CHIPS + 2),
        out_specs=vmem,
        compiler_params=pltpu.CompilerParams(vmem_limit_bytes=VMEM_BYTES),
        cost_estimate=pl.CostEstimate(flops=2 * DP * ROWS * D * ROWS, bytes_accessed=3_000_000, transcendentals=0),
        name="weight_out",
    )(*parts, mine, other)


def fold_kernel(parts_ref, qkv_ref, out_ref):
    total = parts_ref[0, :, : D // 2].astype(jnp.float32)
    for s in range(1, SEQ):
        total = total + parts_ref[s, :, : D // 2].astype(jnp.float32)
    out_ref[:, : D // 2] = total[:8]
    out_ref[:, D // 2 :] = total[8:]
    for h in range(H):
        part = parts_ref[h, :, D // 2 :].astype(jnp.float32)
        qkv_ref[:, h * 3 * HD : (h + 1) * 3 * HD] = jnp.concatenate([part[:8], part[8:, :HD]], axis=1)


def fold(parts):
    vmem = pl.BlockSpec(memory_space=pltpu.VMEM)
    return pl.pallas_call(
        fold_kernel,
        out_shape=(
            jax.ShapeDtypeStruct((8, 3 * D), jnp.float32),
            jax.ShapeDtypeStruct((8, D), jnp.float32),
        ),
        in_specs=[vmem],
        out_specs=(vmem, vmem),
        name="fold",
    )(parts)


def shards(nodes, w_qkv, w_out, cotangent, order, block_list, block_count):
    features, upstream = nodes[0], cotangent[0]
    all_nodes = lax.all_gather(features, "seq", axis=0, tiled=True)
    sent, _ = project(features, upstream, w_qkv, w_out)
    head_rows = lax.all_to_all(sent, "seq", 0, 0, tiled=True).reshape(NODES, WIDE)
    upstreams = batches_of(upstream, sent)
    head_out, attn_sent, grads_sent = attention(block_list[0], block_count[0], order, head_rows, upstreams[0])
    attn = lax.all_to_all(attn_sent, "seq", 0, 0, tiled=True)

    part_qkv, grads_sent = weight_qkv(head_out, all_nodes, grads_sent)
    grads = lax.all_to_all(grads_sent, "seq", 0, 0, tiled=True)
    parts = weight_out(over_dp(attn, part_qkv), *upstreams)
    grad_qkv, grad_out = fold(lax.all_to_all(parts, "seq", 0, 0, tiled=True))

    mixed, grad_nodes = finish(features, upstream, attn, grads, w_qkv, w_out)
    return mixed[None], grad_nodes[None], grad_qkv, grad_out


def solution(mesh):
    return jax.shard_map(
        shards,
        mesh=mesh,
        in_specs=(
            P("dp", "seq", None),
            P(),
            P(),
            P("dp", "seq", None),
            P("dp", None),
            P("dp", None, None),
            P("dp", None),
        ),
        out_specs=(
            P("dp", "seq", None),
            P("dp", "seq", None),
            P(("dp", "seq"), None),
            P(("dp", "seq"), None),
        ),
        check_vma=False,
    )
```

```python
import math

import jax
import jax.numpy as jnp
from jax import lax
from jax.experimental import pallas as pl
from jax.experimental.pallas import tpu as pltpu
from jax.sharding import PartitionSpec as P

H = 16
HD = 64
D = 1024
BLK = 64
MAXB = 8
NODES = 2048
NBLK = 32
WIDE = 4 * HD
TILE = 2048
PAIRS = 2
STEPS = (8, 4)
DP = 8
SEQ = 16
ROWS = 128
CHUNK = 512
HALF = ROWS // 2
STEP = 8
FEW = 2
VMEM_BYTES = 60 * 1024 * 1024
EPS = 1e-05
SCALE = 1.0 / math.sqrt(HD)


def contract(a, b, da, db):
    return lax.dot_general(a, b, (((da,), (db,)), ((), ())), preferred_element_type=jnp.float32)


def attention_kernel(
    list_ref, count_ref, ranked_ref, bounds_ref, order_ref, rows_ref, after_ref, out_ref, attn_ref, grads_ref, qg_ref, kv_ref, acc_ref, done_ref, both_ref
):
    low_lanes = lax.broadcasted_iota(jnp.int32, (TILE, 2 * HD), 1) < HD
    one, none = jnp.ones((TILE, 128), jnp.bfloat16), jnp.zeros((TILE, 128), jnp.bfloat16)

    def to_cluster(t, carry):
        start = pl.multiple_of(t * TILE, TILE)
        ordered = jnp.broadcast_to(order_ref[:, pl.ds(start, TILE)], (128, TILE))
        position = jnp.transpose(ordered.astype(jnp.float32)).astype(jnp.int32)
        lanes = lax.broadcasted_iota(jnp.int32, (TILE, 128), 1)
        within = (position % 128 == lanes).astype(jnp.float32).astype(jnp.bfloat16)
        tile_of = (position // 128).astype(jnp.float32).astype(jnp.bfloat16)
        pick = jnp.concatenate(
            [jnp.where(tile_of == jnp.bfloat16(c), within, none) for c in range(NODES // 128)], axis=1
        )
        moved = contract(pick, rows_ref[...], 1, 0)
        first, second = moved[:, : 2 * HD], moved[:, 2 * HD :]
        qg_ref[pl.ds(start, TILE), :] = jnp.where(low_lanes, first * SCALE, second).astype(jnp.bfloat16)
        kv_ref[pl.ds(start, TILE), :] = jnp.where(
            low_lanes, pltpu.roll(first, HD, 1), pltpu.roll(second, HD, 1)
        ).astype(jnp.bfloat16)
        return carry

    lax.fori_loop(0, NODES // TILE, to_cluster, 0)
    acc_ref[...] = jnp.zeros_like(acc_ref)
    block_low = lax.broadcasted_iota(jnp.int32, (BLK, 2 * HD), 1) < HD
    pair_low = lax.broadcasted_iota(jnp.int32, (1, 2 * BLK), 1) < BLK

    def folded(parts, op):
        total = parts[0]
        for part in parts[1:]:
            total = op(total, part)
        return total

    def pair(at, slot, used):
        blocks = (ranked_ref[at], ranked_ref[at + 1])
        starts = [pl.multiple_of(b * BLK, BLK) for b in blocks]
        qg = [qg_ref[pl.ds(s, BLK), :].astype(jnp.float32) for s in starts]
        keys_at = [[pl.multiple_of(list_ref[b, j] * BLK, BLK) for j in range(used)] for b in blocks]
        kv = jnp.concatenate(
            [jnp.concatenate([kv_ref[pl.ds(key, BLK), :] for key in keys], axis=0) for keys in keys_at], axis=1
        )
        zero = jnp.zeros_like(qg[0])
        q0, q1 = (jnp.where(block_low, x, zero) for x in qg)
        g0, g1 = (jnp.where(block_low, zero, x) for x in qg)
        split = jnp.concatenate(
            [
                jnp.concatenate([q0, zero, g0, zero], axis=0),
                jnp.concatenate([zero, q1, zero, g1], axis=0),
            ],
            axis=1,
        ).astype(jnp.bfloat16)
        both_ref[slot, : used * BLK, :] = contract(kv, split, 1, 1)
        counts = jnp.where(pair_low, count_ref[blocks[0]], count_ref[blocks[1]])
        scores = [
            jnp.where(j < counts, both_ref[slot, j * BLK : (j + 1) * BLK, : 2 * BLK], jnp.float32(-1e30))
            for j in range(used)
        ]
        highest = jnp.max(folded(scores, jnp.maximum), axis=0, keepdims=True)
        expo = [jnp.exp(s - highest) for s in scores]
        inverse = 1.0 / jnp.sum(folded(expo, jnp.add), axis=0, keepdims=True)
        grads = [both_ref[slot, j * BLK : (j + 1) * BLK, 2 * BLK :] for j in range(used)]
        probs = [e * inverse for e in expo]
        delta = jnp.sum(folded([g * p for g, p in zip(grads, probs)], jnp.add), axis=0, keepdims=True)
        mixed = jnp.concatenate(
            [
                jnp.concatenate([(p * (g - delta)).astype(jnp.bfloat16), p.astype(jnp.bfloat16)], axis=1)
                for g, p in zip(grads, probs)
            ],
            axis=0,
        )
        crossed = contract(mixed, kv, 0, 0)
        for s, dq, o in (
            (starts[0], crossed[:64, :128], crossed[128:192, :128]),
            (starts[1], crossed[64:128, 128:], crossed[192:, 128:]),
        ):
            done_ref[pl.ds(s, BLK), : 2 * HD] = (dq * SCALE).astype(jnp.bfloat16)
            done_ref[pl.ds(s, BLK), 2 * HD :] = o.astype(jnp.bfloat16)
        return keys_at, contract(mixed, split, 1, 0)

    def grouped(used):
        def per_group(i, carry):
            found = [pair((i * PAIRS + u) * 2, u, used) for u in range(PAIRS)]
            for keys_at, parts in found:
                for c in range(2):
                    for j in range(used):
                        acc_ref[pl.ds(keys_at[c][j], BLK), :] += parts[
                            j * BLK : (j + 1) * BLK, c * 128 : (c + 1) * 128
                        ]
            return carry

        return per_group

    for step, used in enumerate(STEPS):
        lax.fori_loop(bounds_ref[step], bounds_ref[step + 1], grouped(used), 0)

    def assemble(t, carry):
        start = pl.multiple_of(t * TILE, TILE)
        turned = pltpu.roll(acc_ref[pl.ds(start, TILE), :], HD, 1).astype(jnp.bfloat16)
        rows = pl.ds(start, TILE)
        done_ref[rows, : 2 * HD] = jnp.where(low_lanes, done_ref[rows, : 2 * HD], turned)
        done_ref[rows, 2 * HD :] = jnp.where(low_lanes, turned, done_ref[rows, 2 * HD :])
        return carry

    lax.fori_loop(0, NODES // TILE, assemble, 0)
    row = lax.broadcasted_iota(jnp.int32, (128, NODES), 0).astype(jnp.float32).astype(jnp.bfloat16)
    full, empty = jnp.ones_like(row), jnp.zeros_like(row)

    def to_nodes(t, carry):
        start = pl.multiple_of(t * TILE, TILE)
        offsets = [
            jnp.clip(order_ref[...] - start - 128 * c, -1, 128).astype(jnp.float32).astype(jnp.bfloat16)
            for c in range(TILE // 128)
        ]
        pick = jnp.concatenate([jnp.where(row == offset, full, empty) for offset in offsets], axis=0)
        moved = contract(pick, done_ref[...], 1, 0)
        out_ref[pl.ds(start, TILE), :] = moved.astype(jnp.bfloat16)
        for c in range(TILE // ROWS):
            place = t * (TILE // ROWS) + c
            top, bottom = moved[c * ROWS : c * ROWS + HALF], moved[c * ROWS + HALF : (c + 1) * ROWS]
            late_top, late_bottom = top[:, 2 * HD :], bottom[:, 2 * HD :]
            attn_ref[place] = jnp.where(block_low, pltpu.roll(late_top, HD, 1), late_bottom).astype(jnp.bfloat16)
            grads_ref[place] = jnp.concatenate(
                [top[:, : 2 * HD], jnp.where(block_low, late_top, pltpu.roll(late_bottom, HD, 1)), bottom[:, : 2 * HD]],
                axis=1,
            ).astype(jnp.bfloat16)
        return carry

    lax.fori_loop(0, NODES // TILE, to_nodes, 0)


def ranking(counted):
    index = jnp.arange(NBLK)
    ahead = (counted[None, :] > counted[:, None]) | (
        (counted[None, :] == counted[:, None]) & (index[None, :] < index[:, None])
    )
    rank = jnp.sum(ahead.astype(jnp.int32), axis=1)
    ranked = jnp.sum(jnp.where(rank[None, :] == index[:, None], index[None, :], 0), axis=1)
    above = jnp.stack([jnp.sum((counted > limit).astype(jnp.int32)) for limit in STEPS[1:] + (0,)])
    group = 2 * PAIRS
    bounds = jnp.concatenate([jnp.zeros((1,), jnp.int32), (above + group - 1) // group])
    return ranked.astype(jnp.int32), bounds.astype(jnp.int32)


def attention(picked, counted, order, rows, after):
    ranked, bounds = ranking(counted)
    smem = pl.BlockSpec(memory_space=pltpu.SMEM)
    vmem = pl.BlockSpec(memory_space=pltpu.VMEM)
    return pl.pallas_call(
        attention_kernel,
        out_shape=(
            jax.ShapeDtypeStruct((NODES, WIDE), jnp.bfloat16),
            jax.ShapeDtypeStruct((SEQ, HALF, 2 * HD), jnp.bfloat16),
            jax.ShapeDtypeStruct((SEQ, HALF, 6 * HD), jnp.bfloat16),
        ),
        in_specs=[smem, smem, smem, smem, vmem, vmem, pl.BlockSpec(memory_space=pl.ANY)],
        out_specs=(vmem, vmem, vmem),
        scratch_shapes=[
            pltpu.VMEM((NODES, 2 * HD), jnp.bfloat16),
            pltpu.VMEM((NODES, 2 * HD), jnp.bfloat16),
            pltpu.VMEM((NODES, 2 * HD), jnp.float32),
            pltpu.VMEM((NODES, WIDE), jnp.bfloat16),
            pltpu.VMEM((PAIRS, MAXB * BLK, 4 * BLK), jnp.float32),
        ],
        compiler_params=pltpu.CompilerParams(vmem_limit_bytes=VMEM_BYTES),
        cost_estimate=pl.CostEstimate(flops=10_000_000_000, bytes_accessed=4_000_000, transcendentals=1_000_000),
        name="clustered_attention",
    )(picked, counted, ranked, bounds, order, rows, after)


def project_kernel(features_ref, upstream_ref, w_qkv_ref, w_out_ref, sent_ref, normed_ref):
    @pl.when(pl.program_id(0) == 0)
    def _():
        wide = features_ref[...].astype(jnp.float32)
        inv_rms = lax.rsqrt(jnp.mean(wide * wide, axis=-1, keepdims=True) + EPS)
        normed_ref[...] = (wide * inv_rms).astype(jnp.bfloat16)

    packed = contract(normed_ref[...], w_qkv_ref[...], 1, 0)
    grads = contract(upstream_ref[...], w_out_ref[...], 1, 1)
    for k in range(FEW):
        sent_ref[k] = jnp.concatenate(
            [packed[:, k * 3 * HD : (k + 1) * 3 * HD], grads[:, k * HD : (k + 1) * HD]], axis=1
        ).astype(jnp.bfloat16)


def project(features, upstream, w_qkv, w_out):
    whole = pl.BlockSpec((ROWS, D), lambda i: (0, 0))
    return pl.pallas_call(
        project_kernel,
        grid=(H // FEW,),
        out_shape=jax.ShapeDtypeStruct((H, ROWS, WIDE), jnp.bfloat16),
        in_specs=[
            whole,
            whole,
            pl.BlockSpec((D, 3 * FEW * HD), lambda i: (0, i)),
            pl.BlockSpec((FEW * HD, D), lambda i: (i, 0)),
        ],
        out_specs=pl.BlockSpec((FEW, ROWS, WIDE), lambda i: (i, 0, 0)),
        scratch_shapes=[pltpu.VMEM((ROWS, D), jnp.bfloat16)],
        compiler_params=pltpu.CompilerParams(vmem_limit_bytes=VMEM_BYTES),
        cost_estimate=pl.CostEstimate(flops=2 * ROWS * D * 4 * D, bytes_accessed=9_500_000, transcendentals=ROWS),
        name="project",
    )(features, upstream, w_qkv, w_out)


def node_rows(*heads):
    halves = [jnp.concatenate([h[:, lanes] for h in heads], axis=1) for lanes in (slice(0, HD), slice(HD, 2 * HD))]
    return jnp.concatenate(halves, axis=0)


def finish_kernel(features_ref, upstream_ref, attn_ref, grads_ref, w_qkv_ref, w_out_ref, mixed_ref, grad_ref, mixed_acc, grad_acc):
    step = pl.program_id(0)

    @pl.when(step == 0)
    def _():
        mixed_acc[...] = features_ref[...].astype(jnp.float32)
        grad_acc[...] = jnp.zeros_like(grad_acc)

    attn = node_rows(*(attn_ref[k] for k in range(STEP)))
    first, second = [], []
    for k in range(STEP):
        block = grads_ref[k]
        first += [block[:, : 2 * HD], block[:, 2 * HD : 3 * HD]]
        second += [block[:, 4 * HD :], block[:, 3 * HD : 4 * HD]]
    grads = jnp.concatenate([jnp.concatenate(first, axis=1), jnp.concatenate(second, axis=1)], axis=0)
    mixed_acc[...] += contract(attn, w_out_ref[...], 1, 0)
    grad_acc[...] += contract(grads, w_qkv_ref[...], 1, 1)

    @pl.when(step == pl.num_programs(0) - 1)
    def _():
        wide = features_ref[...].astype(jnp.float32)
        inv_rms = lax.rsqrt(jnp.mean(wide * wide, axis=-1, keepdims=True) + EPS)
        grad_normed = grad_acc[...]
        inner = jnp.mean(grad_normed * wide, axis=-1, keepdims=True)
        mixed_ref[...] = mixed_acc[...].astype(jnp.bfloat16)
        grad_ref[...] = (
            upstream_ref[...].astype(jnp.float32)
            + inv_rms * grad_normed
            - wide * inv_rms * inv_rms * inv_rms * inner
        ).astype(jnp.bfloat16)


def finish(features, upstream, attn, grads, w_qkv, w_out):
    whole = pl.BlockSpec((ROWS, D), lambda i: (0, 0))
    return pl.pallas_call(
        finish_kernel,
        grid=(H // STEP,),
        out_shape=(jax.ShapeDtypeStruct((ROWS, D), jnp.bfloat16),) * 2,
        in_specs=[
            whole,
            whole,
            pl.BlockSpec((STEP, HALF, 2 * HD), lambda i: (i, 0, 0)),
            pl.BlockSpec((STEP, HALF, 6 * HD), lambda i: (i, 0, 0)),
            pl.BlockSpec((D, 3 * STEP * HD), lambda i: (0, i)),
            pl.BlockSpec((STEP * HD, D), lambda i: (i, 0)),
        ],
        out_specs=(whole, whole),
        scratch_shapes=[pltpu.VMEM((ROWS, D), jnp.float32)] * 2,
        compiler_params=pltpu.CompilerParams(vmem_limit_bytes=VMEM_BYTES),
        cost_estimate=pl.CostEstimate(flops=2 * ROWS * D * 4 * D, bytes_accessed=10_000_000, transcendentals=ROWS),
        name="finish",
    )(features, upstream, attn, grads, w_qkv, w_out)


CORES = 2
CHIPS = DP // CORES


def stacked(blocks, after):
    def kernel(*refs):
        for k in range(len(blocks)):
            refs[-1][k * ROWS : (k + 1) * ROWS] = refs[k][...]

    vmem = pl.BlockSpec(memory_space=pltpu.VMEM)
    return pl.pallas_call(
        kernel,
        out_shape=jax.ShapeDtypeStruct((len(blocks) * ROWS, D), jnp.bfloat16),
        in_specs=[vmem] * len(blocks) + [pl.BlockSpec(memory_space=pl.ANY)],
        out_specs=vmem,
        compiler_params=pltpu.CompilerParams(vmem_limit_bytes=VMEM_BYTES),
        cost_estimate=pl.CostEstimate(flops=0, bytes_accessed=4 * D * ROWS * len(blocks), transcendentals=0),
        name="stacked",
    )(*blocks, after)


def weight_qkv_kernel(out_ref, nodes_ref, grads_ref, sent_ref, through_ref):
    total = None
    for t in range(NODES // CHUNK):
        rows = slice(t * CHUNK, (t + 1) * CHUNK)
        wide = nodes_ref[rows, :].astype(jnp.float32)
        inv_rms = lax.rsqrt(jnp.mean(wide * wide, axis=-1, keepdims=True) + EPS)
        part = contract(out_ref[rows, : 3 * HD], (wide * inv_rms).astype(jnp.bfloat16), 0, 0)
        total = part if total is None else total + part
    for i in range(DP):
        sent_ref[i] = total[:, i * ROWS : (i + 1) * ROWS].astype(jnp.bfloat16)


def weight_qkv(head_out, all_nodes, grads):
    vmem = pl.BlockSpec(memory_space=pltpu.VMEM)
    anywhere = pl.BlockSpec(memory_space=pl.ANY)
    return pl.pallas_call(
        weight_qkv_kernel,
        out_shape=(
            jax.ShapeDtypeStruct((DP, 3 * HD, ROWS), jnp.bfloat16),
            jax.ShapeDtypeStruct(grads.shape, grads.dtype),
        ),
        in_specs=[vmem, vmem, anywhere],
        out_specs=(vmem, anywhere),
        input_output_aliases={2: 1},
        compiler_params=pltpu.CompilerParams(vmem_limit_bytes=VMEM_BYTES),
        cost_estimate=pl.CostEstimate(flops=2 * NODES * D * 3 * HD, bytes_accessed=6_000_000, transcendentals=0),
        name="weight_qkv",
    )(head_out, all_nodes, grads)


def chips_kernel(attn_ref, qkv_ref, other_attn_ref, other_qkv_ref, *sent_refs):
    me = lax.axis_index("dp")
    y, core = me // CORES, me % CORES
    first = core == 0
    for step, ref in enumerate(sent_refs):
        i = ((y + step) % CHIPS) * CORES + core
        for k in range(2):
            own, other = attn_ref[2 * i + k], other_attn_ref[2 * i + k]
            ref[k * HALF : (k + 1) * HALF] = jnp.where(first, own, other)
            ref[ROWS + k * HALF : ROWS + (k + 1) * HALF] = jnp.where(first, other, own)
        total = qkv_ref[i].astype(jnp.float32) + other_qkv_ref[i].astype(jnp.float32)
        ref[2 * ROWS :] = total.astype(jnp.bfloat16)


def over_dp(attn, part_qkv):
    pairs = [(i, i ^ 1) for i in range(DP)]
    vmem = pl.BlockSpec(memory_space=pltpu.VMEM)
    shape = jax.ShapeDtypeStruct((2 * ROWS + 3 * HD, ROWS), jnp.bfloat16)
    parts = pl.pallas_call(
        chips_kernel,
        out_shape=(shape,) * CHIPS,
        in_specs=[vmem] * 4,
        out_specs=(vmem,) * CHIPS,
        compiler_params=pltpu.CompilerParams(vmem_limit_bytes=VMEM_BYTES),
        cost_estimate=pl.CostEstimate(flops=0, bytes_accessed=2_000_000, transcendentals=0),
        name="chips",
    )(attn, part_qkv, lax.ppermute(attn, "dp", pairs), lax.ppermute(part_qkv, "dp", pairs))
    moved = {step: lax.ppermute(parts[step], "dp", chip_shift(step)) for step in (2, 1, 3)}
    return parts[0], moved[2], moved[1], moved[3]


def chip_shift(step):
    return [(i, (i + step * CORES) % DP) for i in range(DP)]


def batches_of(block, after):
    moved = [lax.ppermute(block, "dp", chip_shift(step)) for step in (1, 2, 3)]
    mine = stacked((block, *moved), after)
    return mine, lax.ppermute(mine, "dp", [(i, i ^ 1) for i in range(DP)])


def weight_out_kernel(*refs):
    parts, (mine_ref, other_ref, sent_ref) = (refs[0], refs[2], refs[1], refs[3]), refs[CHIPS:]
    core = lax.axis_index("dp") % CORES
    total, mine, other = None, [], []
    for ref in parts:
        qkv = ref[2 * ROWS :].astype(jnp.float32)
        total = qkv if total is None else total + qkv
        attn = [node_rows(ref[c * ROWS : c * ROWS + HALF], ref[c * ROWS + HALF : (c + 1) * ROWS]) for c in range(CORES)]
        mine.append(jnp.where(core == 0, attn[0], attn[1]))
        other.append(jnp.where(core == 0, attn[1], attn[0]))
    out = contract(jnp.concatenate(mine, axis=0), mine_ref[...], 0, 0)
    out += contract(jnp.concatenate(other, axis=0), other_ref[...], 0, 0)
    qkv = jnp.transpose(total)
    nothing = jnp.zeros((8, HD), jnp.float32)
    for s in range(SEQ):
        rows = slice(s * 8, (s + 1) * 8)
        sent_ref[s] = jnp.concatenate(
            [
                jnp.concatenate([out[rows, : D // 2], out[rows, D // 2 :]], axis=0),
                jnp.concatenate(
                    [qkv[rows, : 2 * HD], jnp.concatenate([qkv[rows, 2 * HD :], nothing], axis=1)], axis=0
                ),
            ],
            axis=1,
        ).astype(jnp.bfloat16)


def weight_out(parts, mine, other):
    vmem = pl.BlockSpec(memory_space=pltpu.VMEM)
    return pl.pallas_call(
        weight_out_kernel,
        out_shape=jax.ShapeDtypeStruct((SEQ, 16, D // 2 + 2 * HD), jnp.bfloat16),
        in_specs=[vmem] * (CHIPS + 2),
        out_specs=vmem,
        compiler_params=pltpu.CompilerParams(vmem_limit_bytes=VMEM_BYTES),
        cost_estimate=pl.CostEstimate(flops=2 * DP * ROWS * D * ROWS, bytes_accessed=3_000_000, transcendentals=0),
        name="weight_out",
    )(*parts, mine, other)


def fold_kernel(parts_ref, qkv_ref, out_ref):
    total = parts_ref[0, :, : D // 2].astype(jnp.float32)
    for s in range(1, SEQ):
        total = total + parts_ref[s, :, : D // 2].astype(jnp.float32)
    out_ref[:, : D // 2] = total[:8]
    out_ref[:, D // 2 :] = total[8:]
    for h in range(H):
        part = parts_ref[h, :, D // 2 :].astype(jnp.float32)
        qkv_ref[:, h * 3 * HD : (h + 1) * 3 * HD] = jnp.concatenate([part[:8], part[8:, :HD]], axis=1)


def fold(parts):
    vmem = pl.BlockSpec(memory_space=pltpu.VMEM)
    return pl.pallas_call(
        fold_kernel,
        out_shape=(
            jax.ShapeDtypeStruct((8, 3 * D), jnp.float32),
            jax.ShapeDtypeStruct((8, D), jnp.float32),
        ),
        in_specs=[vmem],
        out_specs=(vmem, vmem),
        name="fold",
    )(parts)


def shards(nodes, w_qkv, w_out, cotangent, order, block_list, block_count):
    features, upstream = nodes[0], cotangent[0]
    all_nodes = lax.all_gather(features, "seq", axis=0, tiled=True)
    sent = project(features, upstream, w_qkv, w_out)
    head_rows = lax.all_to_all(sent, "seq", 0, 0, tiled=True).reshape(NODES, WIDE)
    upstreams = batches_of(upstream, sent)
    head_out, attn_sent, grads_sent = attention(block_list[0], block_count[0], order, head_rows, upstreams[0])
    attn = lax.all_to_all(attn_sent, "seq", 0, 0, tiled=True)

    part_qkv, grads_sent = weight_qkv(head_out, all_nodes, grads_sent)
    grads = lax.all_to_all(grads_sent, "seq", 0, 0, tiled=True)
    parts = weight_out(over_dp(attn, part_qkv), *upstreams)
    grad_qkv, grad_out = fold(lax.all_to_all(parts, "seq", 0, 0, tiled=True))

    mixed, grad_nodes = finish(features, upstream, attn, grads, w_qkv, w_out)
    return mixed[None], grad_nodes[None], grad_qkv, grad_out


def solution(mesh):
    return jax.shard_map(
        shards,
        mesh=mesh,
        in_specs=(
            P("dp", "seq", None),
            P(),
            P(),
            P("dp", "seq", None),
            P("dp", None),
            P("dp", None, None),
            P("dp", None),
        ),
        out_specs=(
            P("dp", "seq", None),
            P("dp", "seq", None),
            P(("dp", "seq"), None),
            P(("dp", "seq"), None),
        ),
        check_vma=False,
    )
```

```python
import math

import jax
import jax.numpy as jnp
from jax import lax
from jax.experimental import pallas as pl
from jax.experimental.pallas import tpu as pltpu
from jax.sharding import PartitionSpec as P

H = 16
HD = 64
D = 1024
BLK = 64
MAXB = 8
NODES = 2048
NBLK = 32
WIDE = 4 * HD
TILE = 2048
PAIRS = 2
STEPS = (8, 4)
DP = 8
SEQ = 16
ROWS = 128
CHUNK = 512
HALF = ROWS // 2
STEP = 8
FEW = 2
VMEM_BYTES = 60 * 1024 * 1024
EPS = 1e-05
SCALE = 1.0 / math.sqrt(HD)


def contract(a, b, da, db):
    return lax.dot_general(a, b, (((da,), (db,)), ((), ())), preferred_element_type=jnp.float32)


def attention_kernel(
    list_ref, count_ref, ranked_ref, bounds_ref, order_ref, rows_ref, after_ref, out_ref, attn_ref, grads_ref, qg_ref, kv_ref, acc_ref, done_ref, both_ref
):
    low_lanes = lax.broadcasted_iota(jnp.int32, (TILE, 2 * HD), 1) < HD
    one, none = jnp.ones((TILE, 128), jnp.bfloat16), jnp.zeros((TILE, 128), jnp.bfloat16)

    def to_cluster(t, carry):
        start = pl.multiple_of(t * TILE, TILE)
        ordered = jnp.broadcast_to(order_ref[:, pl.ds(start, TILE)], (128, TILE))
        position = jnp.transpose(ordered.astype(jnp.float32)).astype(jnp.int32)
        lanes = lax.broadcasted_iota(jnp.int32, (TILE, 128), 1)
        within = (position % 128 == lanes).astype(jnp.float32).astype(jnp.bfloat16)
        tile_of = (position // 128).astype(jnp.float32).astype(jnp.bfloat16)
        pick = jnp.concatenate(
            [jnp.where(tile_of == jnp.bfloat16(c), within, none) for c in range(NODES // 128)], axis=1
        )
        moved = contract(pick, rows_ref[...], 1, 0)
        first, second = moved[:, : 2 * HD], moved[:, 2 * HD :]
        qg_ref[pl.ds(start, TILE), :] = jnp.where(low_lanes, first * SCALE, second).astype(jnp.bfloat16)
        kv_ref[pl.ds(start, TILE), :] = jnp.where(
            low_lanes, pltpu.roll(first, HD, 1), pltpu.roll(second, HD, 1)
        ).astype(jnp.bfloat16)
        return carry

    lax.fori_loop(0, NODES // TILE, to_cluster, 0)
    acc_ref[...] = jnp.zeros_like(acc_ref)
    block_low = lax.broadcasted_iota(jnp.int32, (BLK, 2 * HD), 1) < HD
    pair_low = lax.broadcasted_iota(jnp.int32, (1, 2 * BLK), 1) < BLK

    def folded(parts, op):
        total = parts[0]
        for part in parts[1:]:
            total = op(total, part)
        return total

    def pair(at, slot, used):
        blocks = (ranked_ref[at], ranked_ref[at + 1])
        starts = [pl.multiple_of(b * BLK, BLK) for b in blocks]
        qg = [qg_ref[pl.ds(s, BLK), :].astype(jnp.float32) for s in starts]
        keys_at = [[pl.multiple_of(list_ref[b, j] * BLK, BLK) for j in range(used)] for b in blocks]
        kv = jnp.concatenate(
            [jnp.concatenate([kv_ref[pl.ds(key, BLK), :] for key in keys], axis=0) for keys in keys_at], axis=1
        )
        zero = jnp.zeros_like(qg[0])
        q0, q1 = (jnp.where(block_low, x, zero) for x in qg)
        g0, g1 = (jnp.where(block_low, zero, x) for x in qg)
        split = jnp.concatenate(
            [
                jnp.concatenate([q0, zero, g0, zero], axis=0),
                jnp.concatenate([zero, q1, zero, g1], axis=0),
            ],
            axis=1,
        ).astype(jnp.bfloat16)
        both_ref[slot, : used * BLK, :] = contract(kv, split, 1, 1)
        counts = jnp.where(pair_low, count_ref[blocks[0]], count_ref[blocks[1]])
        scores = [
            jnp.where(j < counts, both_ref[slot, j * BLK : (j + 1) * BLK, : 2 * BLK], jnp.float32(-1e30))
            for j in range(used)
        ]
        highest = jnp.max(folded(scores, jnp.maximum), axis=0, keepdims=True)
        expo = [jnp.exp(s - highest) for s in scores]
        inverse = 1.0 / jnp.sum(folded(expo, jnp.add), axis=0, keepdims=True)
        grads = [both_ref[slot, j * BLK : (j + 1) * BLK, 2 * BLK :] for j in range(used)]
        probs = [e * inverse for e in expo]
        delta = jnp.sum(folded([g * p for g, p in zip(grads, probs)], jnp.add), axis=0, keepdims=True)
        mixed = jnp.concatenate(
            [
                jnp.concatenate([(p * (g - delta)).astype(jnp.bfloat16), p.astype(jnp.bfloat16)], axis=1)
                for g, p in zip(grads, probs)
            ],
            axis=0,
        )
        crossed = contract(mixed, kv, 0, 0)
        for s, dq, o in (
            (starts[0], crossed[:64, :128], crossed[128:192, :128]),
            (starts[1], crossed[64:128, 128:], crossed[192:, 128:]),
        ):
            done_ref[pl.ds(s, BLK), : 2 * HD] = (dq * SCALE).astype(jnp.bfloat16)
            done_ref[pl.ds(s, BLK), 2 * HD :] = o.astype(jnp.bfloat16)
        return keys_at, contract(mixed, split, 1, 0)

    def grouped(used):
        def per_group(i, carry):
            found = [pair((i * PAIRS + u) * 2, u, used) for u in range(PAIRS)]
            for keys_at, parts in found:
                for c in range(2):
                    for j in range(used):
                        acc_ref[pl.ds(keys_at[c][j], BLK), :] += parts[
                            j * BLK : (j + 1) * BLK, c * 128 : (c + 1) * 128
                        ]
            return carry

        return per_group

    for step, used in enumerate(STEPS):
        lax.fori_loop(bounds_ref[step], bounds_ref[step + 1], grouped(used), 0)

    def assemble(t, carry):
        start = pl.multiple_of(t * TILE, TILE)
        turned = pltpu.roll(acc_ref[pl.ds(start, TILE), :], HD, 1).astype(jnp.bfloat16)
        rows = pl.ds(start, TILE)
        done_ref[rows, : 2 * HD] = jnp.where(low_lanes, done_ref[rows, : 2 * HD], turned)
        done_ref[rows, 2 * HD :] = jnp.where(low_lanes, turned, done_ref[rows, 2 * HD :])
        return carry

    lax.fori_loop(0, NODES // TILE, assemble, 0)
    row = lax.broadcasted_iota(jnp.int32, (128, NODES), 0).astype(jnp.float32).astype(jnp.bfloat16)
    full, empty = jnp.ones_like(row), jnp.zeros_like(row)

    def to_nodes(t, carry):
        start = pl.multiple_of(t * TILE, TILE)
        offsets = [
            jnp.clip(order_ref[...] - start - 128 * c, -1, 128).astype(jnp.float32).astype(jnp.bfloat16)
            for c in range(TILE // 128)
        ]
        pick = jnp.concatenate([jnp.where(row == offset, full, empty) for offset in offsets], axis=0)
        moved = contract(pick, done_ref[...], 1, 0)
        out_ref[pl.ds(start, TILE), :] = moved.astype(jnp.bfloat16)
        for c in range(TILE // ROWS):
            place = t * (TILE // ROWS) + c
            top, bottom = moved[c * ROWS : c * ROWS + HALF], moved[c * ROWS + HALF : (c + 1) * ROWS]
            late_top, late_bottom = top[:, 2 * HD :], bottom[:, 2 * HD :]
            attn_ref[place] = jnp.where(block_low, pltpu.roll(late_top, HD, 1), late_bottom).astype(jnp.bfloat16)
            grads_ref[place] = jnp.concatenate(
                [top[:, : 2 * HD], jnp.where(block_low, late_top, pltpu.roll(late_bottom, HD, 1)), bottom[:, : 2 * HD]],
                axis=1,
            ).astype(jnp.bfloat16)
        return carry

    lax.fori_loop(0, NODES // TILE, to_nodes, 0)


def ranking(counted):
    index = jnp.arange(NBLK)
    ahead = (counted[None, :] > counted[:, None]) | (
        (counted[None, :] == counted[:, None]) & (index[None, :] < index[:, None])
    )
    rank = jnp.sum(ahead.astype(jnp.int32), axis=1)
    ranked = jnp.sum(jnp.where(rank[None, :] == index[:, None], index[None, :], 0), axis=1)
    above = jnp.stack([jnp.sum((counted > limit).astype(jnp.int32)) for limit in STEPS[1:] + (0,)])
    group = 2 * PAIRS
    bounds = jnp.concatenate([jnp.zeros((1,), jnp.int32), (above + group - 1) // group])
    return ranked.astype(jnp.int32), bounds.astype(jnp.int32)


def attention(picked, counted, order, rows, after):
    ranked, bounds = ranking(counted)
    smem = pl.BlockSpec(memory_space=pltpu.SMEM)
    vmem = pl.BlockSpec(memory_space=pltpu.VMEM)
    return pl.pallas_call(
        attention_kernel,
        out_shape=(
            jax.ShapeDtypeStruct((NODES, WIDE), jnp.bfloat16),
            jax.ShapeDtypeStruct((SEQ, HALF, 2 * HD), jnp.bfloat16),
            jax.ShapeDtypeStruct((SEQ, HALF, 6 * HD), jnp.bfloat16),
        ),
        in_specs=[smem, smem, smem, smem, vmem, vmem, pl.BlockSpec(memory_space=pl.ANY)],
        out_specs=(vmem, vmem, vmem),
        scratch_shapes=[
            pltpu.VMEM((NODES, 2 * HD), jnp.bfloat16),
            pltpu.VMEM((NODES, 2 * HD), jnp.bfloat16),
            pltpu.VMEM((NODES, 2 * HD), jnp.float32),
            pltpu.VMEM((NODES, WIDE), jnp.bfloat16),
            pltpu.VMEM((PAIRS, MAXB * BLK, 4 * BLK), jnp.float32),
        ],
        compiler_params=pltpu.CompilerParams(vmem_limit_bytes=VMEM_BYTES),
        cost_estimate=pl.CostEstimate(flops=10_000_000_000, bytes_accessed=4_000_000, transcendentals=1_000_000),
        name="clustered_attention",
    )(picked, counted, ranked, bounds, order, rows, after)


def project_kernel(features_ref, upstream_ref, w_qkv_ref, w_out_ref, sent_ref, normed_ref):
    @pl.when(pl.program_id(0) == 0)
    def _():
        wide = features_ref[...].astype(jnp.float32)
        inv_rms = lax.rsqrt(jnp.mean(wide * wide, axis=-1, keepdims=True) + EPS)
        normed_ref[...] = (wide * inv_rms).astype(jnp.bfloat16)

    packed = contract(normed_ref[...], w_qkv_ref[...], 1, 0)
    grads = contract(upstream_ref[...], w_out_ref[...], 1, 1)
    for k in range(FEW):
        sent_ref[k] = jnp.concatenate(
            [packed[:, k * 3 * HD : (k + 1) * 3 * HD], grads[:, k * HD : (k + 1) * HD]], axis=1
        ).astype(jnp.bfloat16)


def project(features, upstream, w_qkv, w_out):
    whole = pl.BlockSpec((ROWS, D), lambda i: (0, 0))
    return pl.pallas_call(
        project_kernel,
        grid=(H // FEW,),
        out_shape=(
            jax.ShapeDtypeStruct((H, ROWS, WIDE), jnp.bfloat16),
            jax.ShapeDtypeStruct((ROWS, D), jnp.bfloat16),
        ),
        in_specs=[
            whole,
            whole,
            pl.BlockSpec((D, 3 * FEW * HD), lambda i: (0, i)),
            pl.BlockSpec((FEW * HD, D), lambda i: (i, 0)),
        ],
        out_specs=(pl.BlockSpec((FEW, ROWS, WIDE), lambda i: (i, 0, 0)), whole),
        compiler_params=pltpu.CompilerParams(vmem_limit_bytes=VMEM_BYTES),
        cost_estimate=pl.CostEstimate(flops=2 * ROWS * D * 4 * D, bytes_accessed=9_500_000, transcendentals=ROWS),
        name="project",
    )(features, upstream, w_qkv, w_out)


def node_rows(*heads):
    halves = [jnp.concatenate([h[:, lanes] for h in heads], axis=1) for lanes in (slice(0, HD), slice(HD, 2 * HD))]
    return jnp.concatenate(halves, axis=0)


def finish_kernel(features_ref, upstream_ref, attn_ref, grads_ref, w_qkv_ref, w_out_ref, mixed_ref, grad_ref, mixed_acc, grad_acc):
    step = pl.program_id(0)

    @pl.when(step == 0)
    def _():
        mixed_acc[...] = features_ref[...].astype(jnp.float32)
        grad_acc[...] = jnp.zeros_like(grad_acc)

    attn = node_rows(*(attn_ref[k] for k in range(STEP)))
    first, second = [], []
    for k in range(STEP):
        block = grads_ref[k]
        first += [block[:, : 2 * HD], block[:, 2 * HD : 3 * HD]]
        second += [block[:, 4 * HD :], block[:, 3 * HD : 4 * HD]]
    grads = jnp.concatenate([jnp.concatenate(first, axis=1), jnp.concatenate(second, axis=1)], axis=0)
    mixed_acc[...] += contract(attn, w_out_ref[...], 1, 0)
    grad_acc[...] += contract(grads, w_qkv_ref[...], 1, 1)

    @pl.when(step == pl.num_programs(0) - 1)
    def _():
        wide = features_ref[...].astype(jnp.float32)
        inv_rms = lax.rsqrt(jnp.mean(wide * wide, axis=-1, keepdims=True) + EPS)
        grad_normed = grad_acc[...]
        inner = jnp.mean(grad_normed * wide, axis=-1, keepdims=True)
        mixed_ref[...] = mixed_acc[...].astype(jnp.bfloat16)
        grad_ref[...] = (
            upstream_ref[...].astype(jnp.float32)
            + inv_rms * grad_normed
            - wide * inv_rms * inv_rms * inv_rms * inner
        ).astype(jnp.bfloat16)


def finish(features, upstream, attn, grads, w_qkv, w_out):
    whole = pl.BlockSpec((ROWS, D), lambda i: (0, 0))
    return pl.pallas_call(
        finish_kernel,
        grid=(H // STEP,),
        out_shape=(jax.ShapeDtypeStruct((ROWS, D), jnp.bfloat16),) * 2,
        in_specs=[
            whole,
            whole,
            pl.BlockSpec((STEP, HALF, 2 * HD), lambda i: (i, 0, 0)),
            pl.BlockSpec((STEP, HALF, 6 * HD), lambda i: (i, 0, 0)),
            pl.BlockSpec((D, 3 * STEP * HD), lambda i: (0, i)),
            pl.BlockSpec((STEP * HD, D), lambda i: (i, 0)),
        ],
        out_specs=(whole, whole),
        scratch_shapes=[pltpu.VMEM((ROWS, D), jnp.float32)] * 2,
        compiler_params=pltpu.CompilerParams(vmem_limit_bytes=VMEM_BYTES),
        cost_estimate=pl.CostEstimate(flops=2 * ROWS * D * 4 * D, bytes_accessed=10_000_000, transcendentals=ROWS),
        name="finish",
    )(features, upstream, attn, grads, w_qkv, w_out)


CORES = 2
CHIPS = DP // CORES


def stacked(blocks, after):
    def kernel(*refs):
        for k in range(len(blocks)):
            refs[-1][k * ROWS : (k + 1) * ROWS] = refs[k][...]

    vmem = pl.BlockSpec(memory_space=pltpu.VMEM)
    return pl.pallas_call(
        kernel,
        out_shape=jax.ShapeDtypeStruct((len(blocks) * ROWS, D), jnp.bfloat16),
        in_specs=[vmem] * len(blocks) + [pl.BlockSpec(memory_space=pl.ANY)],
        out_specs=vmem,
        compiler_params=pltpu.CompilerParams(vmem_limit_bytes=VMEM_BYTES),
        cost_estimate=pl.CostEstimate(flops=0, bytes_accessed=4 * D * ROWS * len(blocks), transcendentals=0),
        name="stacked",
    )(*blocks, after)


def weight_qkv_kernel(out_ref, nodes_ref, sent_ref):
    total = None
    for t in range(NODES // CHUNK):
        rows = slice(t * CHUNK, (t + 1) * CHUNK)
        wide = nodes_ref[rows, :].astype(jnp.float32)
        inv_rms = lax.rsqrt(jnp.mean(wide * wide, axis=-1, keepdims=True) + EPS)
        part = contract(out_ref[rows, : 3 * HD], (wide * inv_rms).astype(jnp.bfloat16), 0, 0)
        total = part if total is None else total + part
    for i in range(DP):
        sent_ref[i] = total[:, i * ROWS : (i + 1) * ROWS].astype(jnp.bfloat16)


def weight_qkv(head_out, all_nodes):
    vmem = pl.BlockSpec(memory_space=pltpu.VMEM)
    return pl.pallas_call(
        weight_qkv_kernel,
        out_shape=jax.ShapeDtypeStruct((DP, 3 * HD, ROWS), jnp.bfloat16),
        in_specs=[vmem, vmem],
        out_specs=vmem,
        compiler_params=pltpu.CompilerParams(vmem_limit_bytes=VMEM_BYTES),
        cost_estimate=pl.CostEstimate(flops=2 * NODES * D * 3 * HD, bytes_accessed=6_000_000, transcendentals=0),
        name="weight_qkv",
    )(head_out, all_nodes)


def chips_kernel(attn_ref, qkv_ref, other_attn_ref, other_qkv_ref, grads_ref, *sent_refs):
    me = lax.axis_index("dp")
    y, core = me // CORES, me % CORES
    first = core == 0
    for step, ref in enumerate(sent_refs[:CHIPS]):
        i = ((y + step) % CHIPS) * CORES + core
        for k in range(2):
            own, other = attn_ref[2 * i + k], other_attn_ref[2 * i + k]
            ref[k * HALF : (k + 1) * HALF] = jnp.where(first, own, other)
            ref[ROWS + k * HALF : ROWS + (k + 1) * HALF] = jnp.where(first, other, own)
        total = qkv_ref[i].astype(jnp.float32) + other_qkv_ref[i].astype(jnp.float32)
        ref[2 * ROWS :] = total.astype(jnp.bfloat16)


def over_dp(attn, part_qkv, grads):
    pairs = [(i, i ^ 1) for i in range(DP)]
    vmem = pl.BlockSpec(memory_space=pltpu.VMEM)
    anywhere = pl.BlockSpec(memory_space=pl.ANY)
    shape = jax.ShapeDtypeStruct((2 * ROWS + 3 * HD, ROWS), jnp.bfloat16)
    *parts, grads = pl.pallas_call(
        chips_kernel,
        out_shape=(shape,) * CHIPS + (jax.ShapeDtypeStruct(grads.shape, grads.dtype),),
        in_specs=[vmem] * 4 + [anywhere],
        out_specs=(vmem,) * CHIPS + (anywhere,),
        input_output_aliases={4: CHIPS},
        compiler_params=pltpu.CompilerParams(vmem_limit_bytes=VMEM_BYTES),
        cost_estimate=pl.CostEstimate(flops=0, bytes_accessed=2_000_000, transcendentals=0),
        name="chips",
    )(attn, part_qkv, lax.ppermute(attn, "dp", pairs), lax.ppermute(part_qkv, "dp", pairs), grads)
    return (parts[0], *(lax.ppermute(parts[step], "dp", chip_shift(step)) for step in (1, 2, 3))), grads


def chip_shift(step):
    return [(i, (i + step * CORES) % DP) for i in range(DP)]


def batches_of(block, after):
    moved = [lax.ppermute(block, "dp", chip_shift(step)) for step in (1, 2, 3)]
    mine = stacked((block, *moved), after)
    return mine, lax.ppermute(mine, "dp", [(i, i ^ 1) for i in range(DP)])


def weight_out_kernel(*refs):
    parts, (mine_ref, other_ref, _, sent_ref) = refs[:CHIPS], refs[CHIPS:]
    core = lax.axis_index("dp") % CORES
    total, mine, other = None, [], []
    for ref in parts:
        qkv = ref[2 * ROWS :].astype(jnp.float32)
        total = qkv if total is None else total + qkv
        attn = [node_rows(ref[c * ROWS : c * ROWS + HALF], ref[c * ROWS + HALF : (c + 1) * ROWS]) for c in range(CORES)]
        mine.append(jnp.where(core == 0, attn[0], attn[1]))
        other.append(jnp.where(core == 0, attn[1], attn[0]))
    out = contract(jnp.concatenate(mine, axis=0), mine_ref[...], 0, 0)
    out += contract(jnp.concatenate(other, axis=0), other_ref[...], 0, 0)
    qkv = jnp.transpose(total)
    nothing = jnp.zeros((8, HD), jnp.float32)
    for s in range(SEQ):
        rows = slice(s * 8, (s + 1) * 8)
        sent_ref[s] = jnp.concatenate(
            [
                jnp.concatenate([out[rows, : D // 2], out[rows, D // 2 :]], axis=0),
                jnp.concatenate(
                    [qkv[rows, : 2 * HD], jnp.concatenate([qkv[rows, 2 * HD :], nothing], axis=1)], axis=0
                ),
            ],
            axis=1,
        ).astype(jnp.bfloat16)


def weight_out(parts, mine, other, after):
    vmem = pl.BlockSpec(memory_space=pltpu.VMEM)
    return pl.pallas_call(
        weight_out_kernel,
        out_shape=jax.ShapeDtypeStruct((SEQ, 16, D // 2 + 2 * HD), jnp.bfloat16),
        in_specs=[vmem] * (CHIPS + 2) + [pl.BlockSpec(memory_space=pl.ANY)],
        out_specs=vmem,
        compiler_params=pltpu.CompilerParams(vmem_limit_bytes=VMEM_BYTES),
        cost_estimate=pl.CostEstimate(flops=2 * DP * ROWS * D * ROWS, bytes_accessed=3_000_000, transcendentals=0),
        name="weight_out",
    )(*parts, mine, other, after)


def fold_kernel(parts_ref, qkv_ref, out_ref):
    total = parts_ref[0, :, : D // 2].astype(jnp.float32)
    for s in range(1, SEQ):
        total = total + parts_ref[s, :, : D // 2].astype(jnp.float32)
    out_ref[:, : D // 2] = total[:8]
    out_ref[:, D // 2 :] = total[8:]
    for h in range(H):
        part = parts_ref[h, :, D // 2 :].astype(jnp.float32)
        qkv_ref[:, h * 3 * HD : (h + 1) * 3 * HD] = jnp.concatenate([part[:8], part[8:, :HD]], axis=1)


def fold(parts):
    vmem = pl.BlockSpec(memory_space=pltpu.VMEM)
    return pl.pallas_call(
        fold_kernel,
        out_shape=(
            jax.ShapeDtypeStruct((8, 3 * D), jnp.float32),
            jax.ShapeDtypeStruct((8, D), jnp.float32),
        ),
        in_specs=[vmem],
        out_specs=(vmem, vmem),
        name="fold",
    )(parts)


def shards(nodes, w_qkv, w_out, cotangent, order, block_list, block_count):
    features, upstream = nodes[0], cotangent[0]
    all_nodes = lax.all_gather(features, "seq", axis=0, tiled=True)
    sent, _ = project(features, upstream, w_qkv, w_out)
    head_rows = lax.all_to_all(sent, "seq", 0, 0, tiled=True).reshape(NODES, WIDE)
    upstreams = batches_of(upstream, sent)
    head_out, attn_sent, grads_sent = attention(block_list[0], block_count[0], order, head_rows, upstreams[0])
    attn = lax.all_to_all(attn_sent, "seq", 0, 0, tiled=True)

    exchanged, grads_sent = over_dp(attn, weight_qkv(head_out, all_nodes), grads_sent)
    grads = lax.all_to_all(grads_sent, "seq", 0, 0, tiled=True)
    parts = weight_out(exchanged, *upstreams, grads)
    grad_qkv, grad_out = fold(lax.all_to_all(parts, "seq", 0, 0, tiled=True))

    mixed, grad_nodes = finish(features, upstream, attn, grads, w_qkv, w_out)
    return mixed[None], grad_nodes[None], grad_qkv, grad_out


def solution(mesh):
    return jax.shard_map(
        shards,
        mesh=mesh,
        in_specs=(
            P("dp", "seq", None),
            P(),
            P(),
            P("dp", "seq", None),
            P("dp", None),
            P("dp", None, None),
            P("dp", None),
        ),
        out_specs=(
            P("dp", "seq", None),
            P("dp", "seq", None),
            P(("dp", "seq"), None),
            P(("dp", "seq"), None),
        ),
        check_vma=False,
    )
```
